1024 devices in a mesh: rep: 32 (over y_hi, z), exp: 32 (over x, y_lo, core).
Axes of the slice: x: 4, y: 8 (y_hi: 2, y_lo: 4; y = y_hi * 4 + y_lo), z: 16, core: 2. Of those that a mesh axis runs over, the one named last changes fastest.
Arguments:
- tokens: bfloat16 [131072, 2048], P(('rep', 'exp')), may hold values from -6 to 6
- expert_ids: int32 [131072, 8], P(('rep', 'exp')), may hold values from 0 to 127, all different within a row
- route_weights: float32 [131072, 8], P(('rep', 'exp')), may hold values from 0.05 to 1
- w_gate: bfloat16 [32, 2048, 384], P('exp'), may hold values from -0.125 to 0.125
- w_up: bfloat16 [32, 2048, 384], P('exp'), may hold values from -0.125 to 0.125
- w_down: bfloat16 [32, 384, 2048], P('exp'), may hold values from -0.21875 to 0.21875
- pseudo_values: bfloat16 [32, 2048, 2048], P('rep', 'exp'), may hold values from -4 to 4
- block_scales: float32 [32, 2048, 16], P('rep', 'exp'), may hold values from 0.1 to 1.5
- outer_params: float32 [3, 2048, 2048], P(None, 'exp'), may hold values from -6 to 6
- momentum: float32 [2048, 2048], P('exp'), may hold values from -4 to 4
- fragment: int32 [1], replicated, may hold values from 0 to 2
Outputs:
- moe_out: bfloat16 [131072, 2048], P(('rep', 'exp'))
- new_params: float32 [2048, 2048], P('exp')
- new_momentum: float32 [2048, 2048], P('exp')
The draws below stay inside these ranges and needn't reach their ends.
Inputs may be any that keep to these rules, and one draw needn't show every extreme that they name: `expert_ids`: each row names 8 different experts.
All inputs are finite; a program needn't handle non-finite values.
Results may differ from the reference program's by a relative error of at most 0.0085.
Values may be sent and summed in bfloat16 or wider, within the bound.
No kernel may reach another device: no remote copies, remote signals or barrier semaphores. Data moves between devices by JAX's collectives and lax.ppermute only.
A program may use at most 64 MiB of HBM per device.

```python
import math
import jax
import jax.numpy as jnp
from jax import lax

D = 2048
HIDDEN_SIZE = 768
ALL_EXPERTS = 128
TOPK = 8
TOK_DEV = 128
FRAGS = 3
BLOCK = 128
EXPERTS = 16
HALF = 384
CAP = 16
TOKENS = 131072
FRAG_ROWS = 2048
N_REP = 32
N_EXP = 32


def level_of(stream_key, shape, pieces, low, high):
    def one(axis_at, parts):
        steps = jax.random.uniform(jax.random.fold_in(jax.random.fold_in(stream_key, 6), axis_at), (parts,), jnp.float32, low / len(pieces), high / len(pieces))
        return jnp.repeat(jnp.exp(steps), shape[axis_at] // parts).reshape((-1,) + (1,) * (len(shape) - axis_at - 1))

    level = one(*pieces[0])
    for cut in pieces[1:]:
        level = level * one(*cut)
    return level


def picks_of(own_key, rows, count, top, lift):
    ranking = jax.random.permutation(jax.random.fold_in(own_key, 1), count)
    favour = ranking
    for power in range(3):
        favour = favour * favour // count
    favour = favour * lift // count
    chance = jax.random.randint(jax.random.fold_in(own_key, 2), (rows, count), 0, 4096) + favour
    holders = jax.random.permutation(jax.random.fold_in(own_key, 3), rows)[jnp.arange(count) % rows]
    chance = jnp.where(jnp.arange(rows)[:, None] == holders[None, :], 1 << 14, chance)
    priority = chance * count + jnp.arange(count)
    return lax.top_k(priority.astype(jnp.int32), top)[1].astype(jnp.int32)


def scatter_about(stream_key, shape, deviation, reach, cuts=(), kind=jnp.bfloat16):
    values = jax.random.normal(stream_key, shape, jnp.float32) * deviation
    if len(cuts) > 0:
        values = level_of(stream_key, shape, cuts, -0.22, 0.18) * values
    return jnp.clip(values, min=-reach, max=reach).astype(kind)


def setup_inputs(seed: int = 0) -> dict:
    streams_of = jax.random.split(jax.random.key(seed), 12)
    tokens = scatter_about(streams_of[0], (TOKENS, D), 1.0, 6.0, ((0, 1024),))
    expert_ids = picks_of(streams_of[1], TOKENS, ALL_EXPERTS, TOPK, 1024)
    route_weights = jnp.clip(jnp.exp(math.log(1.0) - 2.9957323 * jax.random.uniform(streams_of[2], (TOKENS, TOPK), jnp.float32) ** level_of(streams_of[2], (TOKENS, TOPK), ((0, 1024),), -0.2, 0.2)), 0.05, 1.0)
    w_gate = scatter_about(streams_of[3], (2 * EXPERTS, D, HALF), D ** -0.5, 0.125, ((0, 32),))
    w_up = scatter_about(streams_of[4], (2 * EXPERTS, D, HALF), D ** -0.5, 0.125, ((0, 32),))
    w_down = scatter_about(streams_of[5], (2 * EXPERTS, HALF, D), HIDDEN_SIZE ** -0.5, 0.21875, ((0, 32),))
    pseudo_values = scatter_about(streams_of[6], (N_REP, FRAG_ROWS, D), 1.0, 4.0, ((0, 32), (1, 32)))
    block_scales = jnp.clip(jnp.exp(math.log(1.5) - 2.7080502 * jax.random.uniform(streams_of[7], (N_REP, FRAG_ROWS, D // BLOCK), jnp.float32) ** level_of(streams_of[7], (N_REP, FRAG_ROWS, D // BLOCK), ((0, 32), (1, 32)), -0.2, 0.2)), 0.1, 1.5)
    outer_params = scatter_about(streams_of[8], (FRAGS, FRAG_ROWS, D), 1.0, 6.0, ((1, 32),), jnp.float32)
    momentum = scatter_about(streams_of[9], (FRAG_ROWS, D), 0.5, 4.0, ((0, 32),), jnp.float32)
    fragment = jax.random.randint(streams_of[10], (1,), 0, FRAGS).astype(jnp.int32)
    return dict(tokens=tokens, expert_ids=expert_ids, route_weights=route_weights, w_gate=w_gate, w_up=w_up, w_down=w_down, pseudo_values=pseudo_values, block_scales=block_scales, outer_params=outer_params, momentum=momentum, fragment=fragment)


momentum_rate = 0.9
outer_rate = 0.7


def route_slots(expert_ids, experts, capacity):
    ids = expert_ids.astype(jnp.int32)
    rows_count = ids.shape[0]
    columns = jnp.arange(experts, dtype=jnp.int32)
    onehot = (ids[:, :, None] == columns[None, None, :]).astype(jnp.float32)
    per_token = jnp.sum(onehot, axis=1)
    row_pos = jnp.arange(rows_count, dtype=jnp.int32)
    lower = (row_pos[:, None] > row_pos[None, :]).astype(jnp.float32)
    prefix = jnp.dot(lower, per_token, precision=lax.Precision.HIGHEST, preferred_element_type=jnp.float32)
    rank_float = jnp.sum(onehot * prefix[:, None, :], axis=2)
    rank_in = (rank_float + 0.5).astype(jnp.int32).reshape(-1)
    flat_ids = ids.reshape(-1)
    kept_mask = (flat_ids < experts) & (rank_in < capacity)
    slot_index = jnp.where(kept_mask, flat_ids * capacity + rank_in, experts * capacity)
    return slot_index.astype(jnp.int32)


def build_buffer(tokens, slot_index, experts, capacity, topk):
    count = tokens.shape[0] * topk
    source = (jnp.arange(count, dtype=jnp.int32) // topk + 1).astype(jnp.int32)
    owner = jnp.zeros((experts * capacity + 1,), jnp.int32).at[slot_index].set(source)
    owner = owner[: experts * capacity]
    picked = jnp.take(tokens, jnp.maximum(owner - 1, 0).astype(jnp.int32), axis=0)
    filled = jnp.where((owner > 0)[:, None], picked, jnp.zeros_like(picked))
    return filled.reshape(experts, capacity, tokens.shape[1])


def combine(expert_flat, slot_index, route_weights):
    topk = route_weights.shape[1]
    padded = jnp.concatenate([expert_flat, jnp.zeros((1, expert_flat.shape[1]), expert_flat.dtype)], axis=0)
    slots = slot_index.reshape(-1, topk)
    total = jnp.zeros((slots.shape[0], expert_flat.shape[1]), expert_flat.dtype)
    for choice_idx in range(topk):
        rows_got = jnp.take(padded, slots[:, choice_idx], axis=0)
        total = total + route_weights[:, choice_idx][:, None] * rows_got
    return total.astype(jnp.bfloat16)


def reference(tokens, expert_ids, route_weights, w_gate, w_up, w_down, pseudo_values, block_scales, outer_params, momentum, fragment):
    experts = N_EXP // 2
    tok_all = tokens.reshape(N_REP, N_EXP, TOK_DEV, D)
    ids_all = expert_ids.reshape(N_REP, N_EXP, TOK_DEV, TOPK)
    wts_all = route_weights.reshape(N_REP, N_EXP, TOK_DEV, TOPK)

    def one_replica(packed):
        tok_rep, ids_rep, wts_rep = packed
        slots = jax.vmap(lambda ids: route_slots(ids, experts, CAP))(ids_rep)
        buffers = jax.vmap(lambda tok, slot_index: build_buffer(tok, slot_index, experts, CAP, TOPK))(tok_rep, slots)

        def one_expert(expert):
            inputs = jnp.take(buffers, expert, axis=1).reshape(N_EXP * CAP, D)
            total = jnp.zeros((N_EXP * CAP, D), jnp.float32)
            for half_idx in range(2):
                index = (expert * 2 + half_idx).astype(jnp.int32)
                gate_out = jnp.dot(inputs, jnp.take(w_gate, index, axis=0), preferred_element_type=jnp.float32)
                up_out = jnp.dot(inputs, jnp.take(w_up, index, axis=0), preferred_element_type=jnp.float32)
                hidden = (jax.nn.silu(gate_out) * up_out).astype(jnp.bfloat16)
                partial_value = jnp.dot(hidden, jnp.take(w_down, index, axis=0), preferred_element_type=jnp.float32).astype(jnp.bfloat16)
                total = total + partial_value.astype(jnp.float32)
            return total.reshape(N_EXP, CAP, D)

        outs = lax.map(one_expert, jnp.arange(experts, dtype=jnp.int32))
        outs = jnp.transpose(outs, (1, 0, 2, 3)).reshape(N_EXP, experts * CAP, D)
        return jax.vmap(combine)(outs, slots, wts_rep)

    moe_out = lax.map(one_replica, (tok_all, ids_all, wts_all)).reshape(TOKENS, D)
    blocks = D // BLOCK
    dequant = (pseudo_values.astype(jnp.float32).reshape(N_REP, FRAG_ROWS, blocks, BLOCK) * block_scales[:, :, :, None]).reshape(N_REP, FRAG_ROWS, D)
    delta = jnp.sum(dequant, axis=0) / N_REP
    new_momentum = momentum_rate * momentum + delta
    base = lax.dynamic_index_in_dim(outer_params, fragment[0].astype(jnp.int32), 0, keepdims=False)
    new_params = base - outer_rate * (delta + momentum_rate * new_momentum)
    return moe_out, new_params, new_momentum
```

```python
import functools

import jax
import jax.numpy as jnp
from jax import lax
from jax.experimental import pallas as pl
from jax.experimental.pallas import tpu as pltpu
from jax.sharding import Mesh
from jax.sharding import PartitionSpec as P

CAP = 16

momentum_rate = 0.9
outer_rate = 0.7


def route_kernel(experts, ids_ref, weights_ref, tokens_ref, buffer_ref, combine_ref):
    topk, rows = ids_ref.shape
    ids = ids_ref[...]
    weights = weights_ref[...]
    expert = lax.broadcasted_iota(jnp.int32, (experts, rows), 0)
    named = jnp.zeros((experts, rows), jnp.float32)
    weight = jnp.zeros((experts, rows), jnp.float32)
    for k in range(topk):
        hit = ids[k : k + 1, :] == expert
        named = named + hit.astype(jnp.float32)
        weight = weight + jnp.where(hit, weights[k : k + 1, :], 0.0)
    earlier = lax.broadcasted_iota(jnp.int32, (rows, rows), 0) < lax.broadcasted_iota(
        jnp.int32, (rows, rows), 1
    )
    rank = jnp.dot(
        named.astype(jnp.bfloat16),
        earlier.astype(jnp.bfloat16),
        preferred_element_type=jnp.float32,
    ).astype(jnp.int32)
    rank = jnp.where(named > 0.5, rank, CAP)
    place = lax.broadcasted_iota(jnp.int32, (experts, CAP, rows), 1)
    chosen = rank[:, None, :] == place
    pick = jnp.where(chosen, 1.0, 0.0).reshape(experts * CAP, rows)
    combine_ref[...] = jnp.where(
        chosen, jnp.broadcast_to(weight[:, None, :], chosen.shape), 0.0
    ).reshape(experts * CAP, rows)
    buffer_ref[...] = jnp.dot(
        pick.astype(jnp.bfloat16), tokens_ref[...], preferred_element_type=jnp.float32
    ).astype(jnp.bfloat16)


def route(tokens, expert_ids, route_weights, experts):
    rows, width = tokens.shape
    return pl.pallas_call(
        functools.partial(route_kernel, experts),
        out_shape=(
            jax.ShapeDtypeStruct((experts * CAP, width), jnp.bfloat16),
            jax.ShapeDtypeStruct((experts * CAP, rows), jnp.float32),
        ),
        compiler_params=pltpu.CompilerParams(vmem_limit_bytes=32 * 1024 * 1024),
        name="route",
    )(expert_ids.T, route_weights.T, tokens)


def expert_half(rows, w_gate, w_up, w_down):
    gate_out = jnp.dot(rows, w_gate, preferred_element_type=jnp.float32)
    up_out = jnp.dot(rows, w_up, preferred_element_type=jnp.float32)
    hidden = (jax.nn.silu(gate_out) * up_out).astype(jnp.bfloat16)
    return jnp.dot(hidden, w_down, preferred_element_type=jnp.float32).astype(jnp.bfloat16)


def swap_cores(rows):
    return lax.ppermute(rows, "core", [(0, 1), (1, 0)])


def outer_step(pseudo_values, block_scales, outer_params, momentum, fragment):
    replicas = lax.axis_size("rep")
    _, frag_rows, width = pseudo_values.shape
    blocks = block_scales.shape[2]
    dequant = (
        pseudo_values[0].astype(jnp.float32).reshape(frag_rows, blocks, width // blocks)
        * block_scales[0][:, :, None]
    ).astype(jnp.bfloat16)
    pieces = dequant.reshape(replicas, frag_rows // replicas, width)
    theirs = lax.all_to_all(pieces, "rep", split_axis=0, concat_axis=0, tiled=True)
    piece = jnp.sum(theirs.astype(jnp.float32), axis=0) / replicas
    spread = jnp.broadcast_to(piece.astype(jnp.bfloat16)[None], pieces.shape)
    delta = (
        lax.all_to_all(spread, "rep", split_axis=0, concat_axis=0, tiled=True)
        .reshape(frag_rows, width)
        .astype(jnp.float32)
    )
    base = lax.dynamic_index_in_dim(outer_params, fragment[0], 0, keepdims=False)
    new_momentum = momentum_rate * momentum + delta
    new_params = base - outer_rate * (delta + momentum_rate * new_momentum)
    return (new_params, new_momentum)


def shards(
    tokens,
    expert_ids,
    route_weights,
    w_gate,
    w_up,
    w_down,
    pseudo_values,
    block_scales,
    outer_params,
    momentum,
    fragment,
):
    experts = lax.axis_size("chip")
    width = tokens.shape[1]
    buffer, combine = route(tokens, expert_ids, route_weights, experts)
    mine = lax.all_to_all(
        buffer.reshape(experts, CAP, width), "chip", split_axis=0, concat_axis=0, tiled=True
    ).reshape(experts * CAP, width)
    theirs = swap_cores(mine)
    partial_mine = expert_half(mine, w_gate[0], w_up[0], w_down[0])
    partial_theirs = expert_half(theirs, w_gate[0], w_up[0], w_down[0])
    other_half = swap_cores(partial_theirs)
    total = partial_mine.astype(jnp.float32) + other_half.astype(jnp.float32)
    returned = lax.all_to_all(
        total.astype(jnp.bfloat16).reshape(experts, CAP, width),
        "chip",
        split_axis=0,
        concat_axis=0,
        tiled=True,
    ).reshape(experts * CAP, width)
    high = combine.astype(jnp.bfloat16)
    moe_out = lax.dot_general(
        high, returned, (((0,), (0,)), ((), ())), preferred_element_type=jnp.float32
    ).astype(jnp.bfloat16)
    new_params, new_momentum = outer_step(
        pseudo_values, block_scales, outer_params, momentum, fragment
    )
    return (moe_out, new_params, new_momentum)


def solution(mesh):
    reps, exps = mesh.devices.shape
    fine = Mesh(mesh.devices.reshape(reps, exps // 2, 2), ("rep", "chip", "core"))
    exp = ("chip", "core")
    return jax.shard_map(
        shards,
        mesh=fine,
        in_specs=(
            P(("rep",) + exp, None),
            P(("rep",) + exp, None),
            P(("rep",) + exp, None),
            P(exp, None, None),
            P(exp, None, None),
            P(exp, None, None),
            P("rep", exp, None),
            P("rep", exp, None),
            P(None, exp, None),
            P(exp, None),
            P(),
        ),
        out_specs=(P(("rep",) + exp, None), P(exp, None), P(exp, None)),
        check_vma=False,
    )
```

```python
import functools

import jax
import jax.numpy as jnp
from jax import lax
from jax.experimental import pallas as pl
from jax.experimental.pallas import tpu as pltpu
from jax.sharding import Mesh
from jax.sharding import PartitionSpec as P

CAP = 16
RADIX = 4

momentum_rate = 0.9
outer_rate = 0.7

PARAMS = pltpu.CompilerParams(vmem_limit_bytes=20 * 1024 * 1024)
VMEM = pl.BlockSpec(memory_space=pltpu.VMEM)
SMEM = pl.BlockSpec(memory_space=pltpu.SMEM)


def route_kernel(experts, ids_ref, weights_ref, tokens_ref, buffer_ref, combine_ref):
    topk, rows = ids_ref.shape
    ids = ids_ref[...]
    weights = weights_ref[...]
    expert = lax.broadcasted_iota(jnp.int32, (experts, rows), 0)
    named = jnp.zeros((experts, rows), jnp.float32)
    weight = jnp.zeros((experts, rows), jnp.float32)
    for k in range(topk):
        hit = ids[k : k + 1, :] == expert
        named = named + hit.astype(jnp.float32)
        weight = weight + jnp.where(hit, weights[k : k + 1, :], 0.0)
    earlier = lax.broadcasted_iota(jnp.int32, (rows, rows), 0) < lax.broadcasted_iota(
        jnp.int32, (rows, rows), 1
    )
    rank = jnp.dot(
        named.astype(jnp.bfloat16),
        earlier.astype(jnp.bfloat16),
        preferred_element_type=jnp.float32,
    ).astype(jnp.int32)
    rank = jnp.where(named > 0.5, rank, CAP)
    place = lax.broadcasted_iota(jnp.int32, (experts, CAP, rows), 1)
    chosen = rank[:, None, :] == place
    pick = jnp.where(chosen, 1.0, 0.0).reshape(experts * CAP, rows)
    combine_ref[...] = (
        jnp.where(chosen, jnp.broadcast_to(weight[:, None, :], chosen.shape), 0.0)
        .reshape(experts * CAP, rows)
        .astype(jnp.bfloat16)
    )
    buffer_ref[...] = jnp.dot(
        pick.astype(jnp.bfloat16), tokens_ref[...], preferred_element_type=jnp.float32
    ).astype(jnp.bfloat16)


def route(tokens, expert_ids, route_weights, experts):
    rows, width = tokens.shape
    return pl.pallas_call(
        functools.partial(route_kernel, experts),
        out_shape=(
            jax.ShapeDtypeStruct((experts * CAP, width), jnp.bfloat16),
            jax.ShapeDtypeStruct((experts * CAP, rows), jnp.bfloat16),
        ),
        compiler_params=PARAMS,
        name="route",
    )(expert_ids.T, route_weights.T, tokens)


def expert_kernel(rows_ref, g0_ref, u0_ref, d0_ref, g1_ref, u1_ref, d1_ref, out_ref):
    rows = rows_ref[...]
    total = None
    for gate_ref, up_ref, down_ref in ((g0_ref, u0_ref, d0_ref), (g1_ref, u1_ref, d1_ref)):
        gate = jnp.dot(rows, gate_ref[0], preferred_element_type=jnp.float32)
        up = jnp.dot(rows, up_ref[0], preferred_element_type=jnp.float32)
        hidden = (gate / (1.0 + jnp.exp(-gate)) * up).astype(jnp.bfloat16)
        part = jnp.dot(hidden, down_ref[0], preferred_element_type=jnp.float32)
        total = part if total is None else total + part
    out_ref[...] = total.astype(jnp.bfloat16)


def expert_rows(rows, own, other):
    return pl.pallas_call(
        expert_kernel,
        out_shape=jax.ShapeDtypeStruct(rows.shape, jnp.bfloat16),
        compiler_params=PARAMS,
        name="expert_rows",
    )(rows, *own, *other)


def combine_kernel(combine_ref, rows_ref, out_ref):
    out_ref[...] = lax.dot_general(
        combine_ref[...],
        rows_ref[...],
        (((0,), (0,)), ((), ())),
        preferred_element_type=jnp.float32,
    ).astype(jnp.bfloat16)


def combine_rows(combine, rows):
    return pl.pallas_call(
        combine_kernel,
        out_shape=jax.ShapeDtypeStruct((combine.shape[1], rows.shape[1]), jnp.bfloat16),
        compiler_params=PARAMS,
        name="combine_rows",
    )(combine, rows)


def dequant_kernel(place_ref, values_ref, scales_ref, *out_refs):
    rows, width = out_refs[0].shape
    blocks = scales_ref.shape[0]
    column = lax.broadcasted_iota(jnp.int32, (blocks, width), 1) // (width // blocks)
    spread = (column == lax.broadcasted_iota(jnp.int32, (blocks, width), 0)).astype(jnp.bfloat16)
    scales = scales_ref[...]
    high = scales.astype(jnp.bfloat16)
    rest = scales - high.astype(jnp.float32)
    middle = rest.astype(jnp.bfloat16)
    low = (rest - middle.astype(jnp.float32)).astype(jnp.bfloat16)
    wide = sum(
        lax.dot_general(
            part, spread, (((0,), (0,)), ((), ())), preferred_element_type=jnp.float32
        )
        for part in (high, middle, low)
    )
    whole = (values_ref[0].astype(jnp.float32) * wide).astype(jnp.bfloat16)
    for place in range(RADIX):
        block = whole[place * rows : (place + 1) * rows]
        for step, out_ref in enumerate(out_refs):

            @pl.when((place_ref[0] + step) % RADIX == place)
            def _():
                out_ref[...] = block


def dequant(place, values, scales):
    _, rows, width = values.shape
    part = jax.ShapeDtypeStruct((rows // RADIX, width), jnp.bfloat16)
    return pl.pallas_call(
        dequant_kernel,
        in_specs=[SMEM, VMEM, VMEM],
        out_shape=(part,) * RADIX,
        compiler_params=PARAMS,
        name="dequant",
    )(place, values, scales[0].T)


def add_split_kernel(place_ref, *refs):
    in_refs, out_refs = refs[:RADIX], refs[RADIX:]
    total = sum(ref[...].astype(jnp.float32) for ref in in_refs).astype(jnp.bfloat16)
    width = out_refs[0].shape[1]
    for place in range(RADIX):
        for step, out_ref in enumerate(out_refs):

            @pl.when((place_ref[0] + step) % RADIX == place)
            def _():
                out_ref[...] = total[:, place * width : (place + 1) * width]


def add_split(place, parts):
    rows, width = parts[0].shape
    part = jax.ShapeDtypeStruct((rows, width // RADIX), jnp.bfloat16)
    return pl.pallas_call(
        add_split_kernel,
        in_specs=[SMEM] + [VMEM] * RADIX,
        out_shape=(part,) * RADIX,
        compiler_params=PARAMS,
        name="add_split",
    )(place, *parts)


def add_kernel(*refs):
    refs[-1][...] = sum(ref[...].astype(jnp.float32) for ref in refs[:-1]).astype(jnp.bfloat16)


def add_parts(parts):
    return pl.pallas_call(
        add_kernel,
        out_shape=jax.ShapeDtypeStruct(parts[0].shape, jnp.bfloat16),
        compiler_params=PARAMS,
        name="add_parts",
    )(*parts)


def join_kernel(place_ref, *refs):
    in_refs, out_ref = refs[:RADIX], refs[RADIX]
    width = in_refs[0].shape[1]
    for place in range(RADIX):
        for step, ref in enumerate(in_refs):

            @pl.when((place_ref[0] + RADIX - step) % RADIX == place)
            def _():
                out_ref[:, place * width : (place + 1) * width] = ref[...]


def join(place, parts):
    rows, width = parts[0].shape
    return pl.pallas_call(
        join_kernel,
        in_specs=[SMEM] + [VMEM] * RADIX,
        out_shape=jax.ShapeDtypeStruct((rows, width * RADIX), jnp.bfloat16),
        compiler_params=PARAMS,
        name="join",
    )(place, *parts)


def update_kernel(replicas, fragment_ref, place_ref, *refs):
    part_refs = refs[:RADIX]
    base_ref, momentum_ref, params_out, momentum_out = refs[RADIX:]
    rows = part_refs[0].shape[0]
    for place in range(RADIX):
        for step, ref in enumerate(part_refs):

            @pl.when((place_ref[0] + RADIX - step) % RADIX == place)
            def _():
                span = pl.ds(place * rows, rows)
                delta = ref[...].astype(jnp.float32) / replicas
                new_momentum = momentum_rate * momentum_ref[span, :] + delta
                momentum_out[span, :] = new_momentum
                params_out[span, :] = base_ref[0, span, :] - outer_rate * (
                    delta + momentum_rate * new_momentum
                )


def update(replicas, place, parts, outer_params, momentum, fragment):
    shape = momentum.shape
    part = parts[0].shape

    def whole(block):
        return pl.BlockSpec(block, lambda i, fragment_ref, place_ref: (0,) * len(block))

    return pl.pallas_call(
        functools.partial(update_kernel, replicas),
        grid_spec=pltpu.PrefetchScalarGridSpec(
            num_scalar_prefetch=2,
            grid=(1,),
            in_specs=[whole(part)] * RADIX
            + [
                pl.BlockSpec(
                    (1,) + shape, lambda i, fragment_ref, place_ref: (fragment_ref[0], 0, 0)
                ),
                whole(shape),
            ],
            out_specs=(whole(shape), whole(shape)),
        ),
        out_shape=(
            jax.ShapeDtypeStruct(shape, jnp.float32),
            jax.ShapeDtypeStruct(shape, jnp.float32),
        ),
        compiler_params=PARAMS,
        name="update",
    )(fragment, place, *parts, outer_params, momentum)


def shift(part, axis, step):
    size = lax.axis_size(axis)
    return lax.ppermute(part, axis, [(i, (i + step) % size) for i in range(size)])


def scatter_stage(parts, axis):
    return [parts[0]] + [shift(parts[step], axis, step) for step in range(1, RADIX)]


def gather_stage(part, axis):
    return [part] + [shift(part, axis, step) for step in range(1, RADIX)]


def place_on(axis):
    return lax.axis_index(axis).astype(jnp.int32).reshape(1)


def replica_sum(pseudo_values, block_scales):
    near, far = place_on("z_near"), place_on("z_far")
    parts = scatter_stage(dequant(near, pseudo_values, block_scales), "z_near")
    parts = scatter_stage(add_split(far, parts), "z_far")
    return add_parts(parts)


def outer_step(part, outer_params, momentum, fragment):
    near, far = place_on("z_near"), place_on("z_far")
    part = add_parts([part, shift(part, "y_far", 1)])
    part = join(far, gather_stage(part, "z_far"))
    parts = gather_stage(part, "z_near")
    replicas = lax.axis_size(("y_far", "z_far", "z_near"))
    return update(replicas, near, parts, outer_params, momentum, fragment)


def exchange(rows, experts):
    width = rows.shape[1]
    return lax.all_to_all(
        rows.reshape(experts, CAP, width), "chip", split_axis=0, concat_axis=0, tiled=True
    ).reshape(experts * CAP, width)


def shards(
    tokens,
    expert_ids,
    route_weights,
    w_gate,
    w_up,
    w_down,
    pseudo_values,
    block_scales,
    outer_params,
    momentum,
    fragment,
):
    experts = lax.axis_size("chip")
    buffer, combine = route(tokens, expert_ids, route_weights, experts)
    mine = exchange(buffer, experts)
    own = (w_gate, w_up, w_down)
    other = [shift(w, "core", 1) for w in own]
    part = replica_sum(pseudo_values, block_scales)
    mine, part = lax.optimization_barrier((mine, part))
    returned = exchange(expert_rows(mine, own, other), experts)
    moe_out = combine_rows(combine, returned)
    new_params, new_momentum = outer_step(part, outer_params, momentum, fragment)
    return (moe_out, new_params, new_momentum)


def solution(mesh):
    reps, exps = mesh.devices.shape
    fine = Mesh(
        mesh.devices.reshape(reps // (RADIX * RADIX), RADIX, RADIX, exps // 2, 2),
        ("y_far", "z_far", "z_near", "chip", "core"),
    )
    rep = ("y_far", "z_far", "z_near")
    exp = ("chip", "core")
    return jax.shard_map(
        shards,
        mesh=fine,
        in_specs=(
            P(rep + exp, None),
            P(rep + exp, None),
            P(rep + exp, None),
            P(exp, None, None),
            P(exp, None, None),
            P(exp, None, None),
            P(rep, exp, None),
            P(rep, exp, None),
            P(None, exp, None),
            P(exp, None),
            P(),
        ),
        out_specs=(P(rep + exp, None), P(exp, None), P(exp, None)),
        check_vma=False,
    )
```

```python
import functools

import jax
import jax.numpy as jnp
from jax import lax
from jax.experimental import pallas as pl
from jax.experimental.pallas import tpu as pltpu
from jax.sharding import Mesh
from jax.sharding import PartitionSpec as P

CAP = 16
PIECE_ROWS = 16

momentum_rate = 0.9
outer_rate = 0.7

PARAMS = pltpu.CompilerParams(vmem_limit_bytes=20 * 1024 * 1024)
VMEM = pl.BlockSpec(memory_space=pltpu.VMEM)
SMEM = pl.BlockSpec(memory_space=pltpu.SMEM)


def route_kernel(experts, ids_ref, weights_ref, tokens_ref, buffer_ref, combine_ref):
    topk, rows = ids_ref.shape
    ids = ids_ref[...]
    weights = weights_ref[...]
    expert = lax.broadcasted_iota(jnp.int32, (experts, rows), 0)
    named = jnp.zeros((experts, rows), jnp.float32)
    weight = jnp.zeros((experts, rows), jnp.float32)
    for k in range(topk):
        hit = ids[k : k + 1, :] == expert
        named = named + hit.astype(jnp.float32)
        weight = weight + jnp.where(hit, weights[k : k + 1, :], 0.0)
    earlier = lax.broadcasted_iota(jnp.int32, (rows, rows), 0) < lax.broadcasted_iota(
        jnp.int32, (rows, rows), 1
    )
    rank = jnp.dot(
        named.astype(jnp.bfloat16),
        earlier.astype(jnp.bfloat16),
        preferred_element_type=jnp.float32,
    ).astype(jnp.int32)
    rank = jnp.where(named > 0.5, rank, CAP)
    place = lax.broadcasted_iota(jnp.int32, (experts, CAP, rows), 1)
    chosen = rank[:, None, :] == place
    pick = jnp.where(chosen, 1.0, 0.0).reshape(experts * CAP, rows)
    combine_ref[...] = (
        jnp.where(chosen, jnp.broadcast_to(weight[:, None, :], chosen.shape), 0.0)
        .reshape(experts * CAP, rows)
        .astype(jnp.bfloat16)
    )
    buffer_ref[...] = jnp.dot(
        pick.astype(jnp.bfloat16), tokens_ref[...], preferred_element_type=jnp.float32
    ).astype(jnp.bfloat16)


def route(tokens, expert_ids, route_weights, experts):
    rows, width = tokens.shape
    return pl.pallas_call(
        functools.partial(route_kernel, experts),
        out_shape=(
            jax.ShapeDtypeStruct((experts * CAP, width), jnp.bfloat16),
            jax.ShapeDtypeStruct((experts * CAP, rows), jnp.bfloat16),
        ),
        compiler_params=PARAMS,
        name="route",
    )(expert_ids.T, route_weights.T, tokens)


def expert_kernel(rows_ref, g0_ref, u0_ref, d0_ref, g1_ref, u1_ref, d1_ref, out_ref):
    rows = rows_ref[...]
    total = None
    for gate_ref, up_ref, down_ref in ((g0_ref, u0_ref, d0_ref), (g1_ref, u1_ref, d1_ref)):
        gate = jnp.dot(rows, gate_ref[0], preferred_element_type=jnp.float32)
        up = jnp.dot(rows, up_ref[0], preferred_element_type=jnp.float32)
        hidden = (gate / (1.0 + jnp.exp(-gate)) * up).astype(jnp.bfloat16)
        part = jnp.dot(hidden, down_ref[0], preferred_element_type=jnp.float32)
        total = part if total is None else total + part
    out_ref[...] = total.astype(jnp.bfloat16)


def expert_rows(rows, own, other):
    return pl.pallas_call(
        expert_kernel,
        out_shape=jax.ShapeDtypeStruct(rows.shape, jnp.bfloat16),
        compiler_params=PARAMS,
        name="expert_rows",
    )(rows, *own, *other)


def combine_kernel(combine_ref, rows_ref, out_ref):
    out_ref[...] = lax.dot_general(
        combine_ref[...],
        rows_ref[...],
        (((0,), (0,)), ((), ())),
        preferred_element_type=jnp.float32,
    ).astype(jnp.bfloat16)


def combine_rows(combine, rows):
    return pl.pallas_call(
        combine_kernel,
        out_shape=jax.ShapeDtypeStruct((combine.shape[1], rows.shape[1]), jnp.bfloat16),
        compiler_params=PARAMS,
        name="combine_rows",
    )(combine, rows)


def dequant_kernel(values_ref, scales_ref, out_ref):
    replicas, rows, span = out_ref.shape
    width = values_ref.shape[2]
    blocks = scales_ref.shape[0]
    column = lax.broadcasted_iota(jnp.int32, (blocks, width), 1) // (width // blocks)
    spread = (column == lax.broadcasted_iota(jnp.int32, (blocks, width), 0)).astype(jnp.bfloat16)
    scales = scales_ref[...]
    high = scales.astype(jnp.bfloat16)
    rest = scales - high.astype(jnp.float32)
    middle = rest.astype(jnp.bfloat16)
    low = (rest - middle.astype(jnp.float32)).astype(jnp.bfloat16)
    wide = sum(
        lax.dot_general(
            part, spread, (((0,), (0,)), ((), ())), preferred_element_type=jnp.float32
        )
        for part in (high, middle, low)
    )
    whole = (values_ref[0].astype(jnp.float32) * wide).astype(jnp.bfloat16)
    across = width // span
    for piece in range(replicas):
        row, column = piece // across * rows, piece % across * span
        out_ref[piece] = whole[row : row + rows, column : column + span]


def dequant(values, scales, replicas):
    _, rows, width = values.shape
    shape = (replicas, PIECE_ROWS, rows * width // (replicas * PIECE_ROWS))
    return pl.pallas_call(
        dequant_kernel,
        out_shape=jax.ShapeDtypeStruct(shape, jnp.bfloat16),
        compiler_params=PARAMS,
        name="dequant",
    )(values, scales[0].T)


def total_kernel(parts_ref, out_ref):
    total = jnp.sum(parts_ref[...].astype(jnp.float32), axis=0).astype(jnp.bfloat16)
    out_ref[...] = jnp.broadcast_to(total[None], out_ref.shape)


def total_spread(parts):
    return pl.pallas_call(
        total_kernel,
        out_shape=jax.ShapeDtypeStruct(parts.shape, jnp.bfloat16),
        compiler_params=PARAMS,
        name="total_spread",
    )(parts)


def update_kernel(fragment_ref, totals_ref, base_ref, momentum_ref, params_out, momentum_out):
    replicas, rows, span = totals_ref.shape
    across = momentum_ref.shape[1] // span
    for piece in range(replicas):
        at = (
            pl.ds(piece // across * rows, rows),
            pl.ds(piece % across * span, span),
        )
        delta = totals_ref[piece].astype(jnp.float32) / replicas
        new_momentum = momentum_rate * momentum_ref[at] + delta
        momentum_out[at] = new_momentum
        params_out[at] = base_ref[(0,) + at] - outer_rate * (delta + momentum_rate * new_momentum)


def update(totals, outer_params, momentum, fragment):
    shape = momentum.shape

    def whole(block):
        return pl.BlockSpec(block, lambda i, fragment_ref: (0,) * len(block))

    return pl.pallas_call(
        update_kernel,
        grid_spec=pltpu.PrefetchScalarGridSpec(
            num_scalar_prefetch=1,
            grid=(1,),
            in_specs=[
                whole(totals.shape),
                pl.BlockSpec((1,) + shape, lambda i, fragment_ref: (fragment_ref[0], 0, 0)),
                whole(shape),
            ],
            out_specs=(whole(shape), whole(shape)),
        ),
        out_shape=(
            jax.ShapeDtypeStruct(shape, jnp.float32),
            jax.ShapeDtypeStruct(shape, jnp.float32),
        ),
        compiler_params=PARAMS,
        name="update",
    )(fragment, totals, outer_params, momentum)


def shift(part, axis, step):
    size = lax.axis_size(axis)
    return lax.ppermute(part, axis, [(i, (i + step) % size) for i in range(size)])


def swap_pieces(pieces):
    return lax.all_to_all(pieces, "rep", split_axis=0, concat_axis=0, tiled=True)


def exchange(rows, experts):
    width = rows.shape[1]
    return lax.all_to_all(
        rows.reshape(experts, CAP, width), "chip", split_axis=0, concat_axis=0, tiled=True
    ).reshape(experts * CAP, width)


def shards(
    tokens,
    expert_ids,
    route_weights,
    w_gate,
    w_up,
    w_down,
    pseudo_values,
    block_scales,
    outer_params,
    momentum,
    fragment,
):
    experts = lax.axis_size("chip")
    buffer, combine = route(tokens, expert_ids, route_weights, experts)
    mine = exchange(buffer, experts)
    own = (w_gate, w_up, w_down)
    other = [shift(w, "core", 1) for w in own]
    parts = swap_pieces(dequant(pseudo_values, block_scales, lax.axis_size("rep")))
    mine, parts = lax.optimization_barrier((mine, parts))
    returned = exchange(expert_rows(mine, own, other), experts)
    moe_out = combine_rows(combine, returned)
    totals = swap_pieces(total_spread(parts))
    new_params, new_momentum = update(totals, outer_params, momentum, fragment)
    return (moe_out, new_params, new_momentum)


def solution(mesh):
    reps, exps = mesh.devices.shape
    fine = Mesh(mesh.devices.reshape(reps, exps // 2, 2), ("rep", "chip", "core"))
    exp = ("chip", "core")
    return jax.shard_map(
        shards,
        mesh=fine,
        in_specs=(
            P(("rep",) + exp, None),
            P(("rep",) + exp, None),
            P(("rep",) + exp, None),
            P(exp, None, None),
            P(exp, None, None),
            P(exp, None, None),
            P("rep", exp, None),
            P("rep", exp, None),
            P(None, exp, None),
            P(exp, None),
            P(),
        ),
        out_specs=(P(("rep",) + exp, None), P(exp, None), P(exp, None)),
        check_vma=False,
    )
```

```python
import functools

import jax
import jax.numpy as jnp
from jax import lax
from jax.experimental import pallas as pl
from jax.experimental.pallas import tpu as pltpu
from jax.sharding import Mesh
from jax.sharding import PartitionSpec as P

CAP = 16
RADIX = 4

momentum_rate = 0.9
outer_rate = 0.7

PARAMS = pltpu.CompilerParams(vmem_limit_bytes=20 * 1024 * 1024)
VMEM = pl.BlockSpec(memory_space=pltpu.VMEM)
HBM = pl.BlockSpec(memory_space=pltpu.HBM)
SMEM = pl.BlockSpec(memory_space=pltpu.SMEM)


def route_kernel(experts, ids_ref, weights_ref, tokens_ref, buffer_ref, combine_ref):
    topk, rows = ids_ref.shape
    ids = ids_ref[...]
    weights = weights_ref[...]
    expert = lax.broadcasted_iota(jnp.int32, (experts, rows), 0)
    named = jnp.zeros((experts, rows), jnp.float32)
    weight = jnp.zeros((experts, rows), jnp.float32)
    for k in range(topk):
        hit = ids[k : k + 1, :] == expert
        named = named + hit.astype(jnp.float32)
        weight = weight + jnp.where(hit, weights[k : k + 1, :], 0.0)
    earlier = lax.broadcasted_iota(jnp.int32, (rows, rows), 0) < lax.broadcasted_iota(
        jnp.int32, (rows, rows), 1
    )
    rank = jnp.dot(
        named.astype(jnp.bfloat16),
        earlier.astype(jnp.bfloat16),
        preferred_element_type=jnp.float32,
    ).astype(jnp.int32)
    rank = jnp.where(named > 0.5, rank, CAP)
    place = lax.broadcasted_iota(jnp.int32, (experts, CAP, rows), 1)
    chosen = rank[:, None, :] == place
    pick = jnp.where(chosen, 1.0, 0.0).reshape(experts * CAP, rows)
    combine_ref[...] = (
        jnp.where(chosen, jnp.broadcast_to(weight[:, None, :], chosen.shape), 0.0)
        .reshape(experts * CAP, rows)
        .astype(jnp.bfloat16)
    )
    buffer_ref[...] = jnp.dot(
        pick.astype(jnp.bfloat16), tokens_ref[...], preferred_element_type=jnp.float32
    ).astype(jnp.bfloat16)


def route(tokens, expert_ids, route_weights, experts):
    rows, width = tokens.shape
    return pl.pallas_call(
        functools.partial(route_kernel, experts),
        out_shape=(
            jax.ShapeDtypeStruct((experts * CAP, width), jnp.bfloat16),
            jax.ShapeDtypeStruct((experts * CAP, rows), jnp.bfloat16),
        ),
        compiler_params=PARAMS,
        name="route",
    )(expert_ids.T, route_weights.T, tokens)


def expert_kernel(rows_ref, gate_ref, up_ref, down_ref, *refs):
    sources, out_ref, targets, sems = refs[:3], refs[3], refs[4:7], refs[7]
    fetches = [
        pltpu.make_async_copy(source, target, sems.at[i])
        for i, (source, target) in enumerate(zip(sources, targets))
    ]
    for fetch in fetches:
        fetch.start()
    rows = rows_ref[...]

    def part(gate_ref, up_ref, down_ref, waits):
        for wait in waits[:1]:
            wait.wait()
        gate = jnp.dot(rows, gate_ref[0], preferred_element_type=jnp.float32)
        for wait in waits[1:2]:
            wait.wait()
        up = jnp.dot(rows, up_ref[0], preferred_element_type=jnp.float32)
        hidden = (gate / (1.0 + jnp.exp(-gate)) * up).astype(jnp.bfloat16)
        for wait in waits[2:]:
            wait.wait()
        return jnp.dot(hidden, down_ref[0], preferred_element_type=jnp.float32)

    total = part(gate_ref, up_ref, down_ref, []) + part(*targets, fetches)
    out_ref[...] = total.astype(jnp.bfloat16)


def expert_rows(rows, own, other):
    return pl.pallas_call(
        expert_kernel,
        in_specs=[VMEM] * 4 + [HBM] * 3,
        out_shape=jax.ShapeDtypeStruct(rows.shape, jnp.bfloat16),
        scratch_shapes=[pltpu.VMEM(x.shape, x.dtype) for x in other]
        + [pltpu.SemaphoreType.DMA((3,))],
        compiler_params=PARAMS,
        name="expert_rows",
    )(rows, *own, *other)


def combine_kernel(combine_ref, rows_ref, out_ref):
    out_ref[...] = lax.dot_general(
        combine_ref[...],
        rows_ref[...],
        (((0,), (0,)), ((), ())),
        preferred_element_type=jnp.float32,
    ).astype(jnp.bfloat16)


def combine_rows(combine, rows):
    return pl.pallas_call(
        combine_kernel,
        out_shape=jax.ShapeDtypeStruct((combine.shape[1], rows.shape[1]), jnp.bfloat16),
        compiler_params=PARAMS,
        name="combine_rows",
    )(combine, rows)


def dequant_kernel(place_ref, values_ref, scales_ref, *out_refs):
    rows, width = out_refs[0].shape
    blocks = scales_ref.shape[0]
    column = lax.broadcasted_iota(jnp.int32, (blocks, width), 1) // (width // blocks)
    spread = (column == lax.broadcasted_iota(jnp.int32, (blocks, width), 0)).astype(jnp.bfloat16)
    scales = scales_ref[...]
    high = scales.astype(jnp.bfloat16)
    rest = scales - high.astype(jnp.float32)
    middle = rest.astype(jnp.bfloat16)
    low = (rest - middle.astype(jnp.float32)).astype(jnp.bfloat16)
    wide = sum(
        lax.dot_general(
            part, spread, (((0,), (0,)), ((), ())), preferred_element_type=jnp.float32
        )
        for part in (high, middle, low)
    )
    whole = (values_ref[0].astype(jnp.float32) * wide).astype(jnp.bfloat16)
    for place in range(RADIX):
        block = whole[place * rows : (place + 1) * rows]
        for step, out_ref in enumerate(out_refs):

            @pl.when((place_ref[0] + step) % RADIX == place)
            def _():
                out_ref[...] = block


def dequant(place, values, scales):
    _, rows, width = values.shape
    part = jax.ShapeDtypeStruct((rows // RADIX, width), jnp.bfloat16)
    return pl.pallas_call(
        dequant_kernel,
        in_specs=[SMEM, VMEM, VMEM],
        out_shape=(part,) * RADIX,
        compiler_params=PARAMS,
        name="dequant",
    )(place, values, scales[0].T)


def add_split_kernel(place_ref, *refs):
    in_refs, out_refs = refs[:RADIX], refs[RADIX:]
    total = sum(ref[...].astype(jnp.float32) for ref in in_refs).astype(jnp.bfloat16)
    width = out_refs[0].shape[1]
    for place in range(RADIX):
        for step, out_ref in enumerate(out_refs):

            @pl.when((place_ref[0] + step) % RADIX == place)
            def _():
                out_ref[...] = total[:, place * width : (place + 1) * width]


def add_split(place, parts):
    rows, width = parts[0].shape
    part = jax.ShapeDtypeStruct((rows, width // RADIX), jnp.bfloat16)
    return pl.pallas_call(
        add_split_kernel,
        in_specs=[SMEM] + [VMEM] * RADIX,
        out_shape=(part,) * RADIX,
        compiler_params=PARAMS,
        name="add_split",
    )(place, *parts)


def add_kernel(*refs):
    refs[-1][...] = sum(ref[...].astype(jnp.float32) for ref in refs[:-1]).astype(jnp.bfloat16)


def add_parts(parts):
    return pl.pallas_call(
        add_kernel,
        out_shape=jax.ShapeDtypeStruct(parts[0].shape, jnp.bfloat16),
        compiler_params=PARAMS,
        name="add_parts",
    )(*parts)


def join_kernel(place_ref, *refs):
    in_refs, out_ref = refs[:RADIX], refs[RADIX]
    width = in_refs[0].shape[1]
    for place in range(RADIX):
        for step, ref in enumerate(in_refs):

            @pl.when((place_ref[0] + RADIX - step) % RADIX == place)
            def _():
                out_ref[:, place * width : (place + 1) * width] = ref[...]


def join(place, parts):
    rows, width = parts[0].shape
    return pl.pallas_call(
        join_kernel,
        in_specs=[SMEM] + [VMEM] * RADIX,
        out_shape=jax.ShapeDtypeStruct((rows, width * RADIX), jnp.bfloat16),
        compiler_params=PARAMS,
        name="join",
    )(place, *parts)


def update_kernel(replicas, fragment_ref, place_ref, *refs):
    part_refs = refs[:RADIX]
    base_ref, momentum_ref, params_out, momentum_out = refs[RADIX:]
    rows = part_refs[0].shape[0]
    for place in range(RADIX):
        for step, ref in enumerate(part_refs):

            @pl.when((place_ref[0] + RADIX - step) % RADIX == place)
            def _():
                span = pl.ds(place * rows, rows)
                delta = ref[...].astype(jnp.float32) / replicas
                new_momentum = momentum_rate * momentum_ref[span, :] + delta
                momentum_out[span, :] = new_momentum
                params_out[span, :] = base_ref[0, span, :] - outer_rate * (
                    delta + momentum_rate * new_momentum
                )


def update(replicas, place, parts, outer_params, momentum, fragment):
    shape = momentum.shape
    part = parts[0].shape

    def whole(block):
        return pl.BlockSpec(block, lambda i, fragment_ref, place_ref: (0,) * len(block))

    return pl.pallas_call(
        functools.partial(update_kernel, replicas),
        grid_spec=pltpu.PrefetchScalarGridSpec(
            num_scalar_prefetch=2,
            grid=(1,),
            in_specs=[whole(part)] * RADIX
            + [
                pl.BlockSpec(
                    (1,) + shape, lambda i, fragment_ref, place_ref: (fragment_ref[0], 0, 0)
                ),
                whole(shape),
            ],
            out_specs=(whole(shape), whole(shape)),
        ),
        out_shape=(
            jax.ShapeDtypeStruct(shape, jnp.float32),
            jax.ShapeDtypeStruct(shape, jnp.float32),
        ),
        compiler_params=PARAMS,
        name="update",
    )(fragment, place, *parts, outer_params, momentum)


def shift(part, axis, step):
    size = lax.axis_size(axis)
    return lax.ppermute(part, axis, [(i, (i + step) % size) for i in range(size)])


def scatter_stage(parts, axis):
    return [parts[0]] + [shift(parts[step], axis, step) for step in range(1, RADIX)]


def gather_stage(part, axis):
    return [part] + [shift(part, axis, step) for step in range(1, RADIX)]


def place_on(axis):
    return lax.axis_index(axis).astype(jnp.int32).reshape(1)


def outer_step(part, outer_params, momentum, fragment):
    near, far = place_on("z_near"), place_on("z_far")
    part = join(far, gather_stage(part, "z_far"))
    parts = gather_stage(part, "z_near")
    replicas = lax.axis_size(("y_far", "z_far", "z_near"))
    return update(replicas, near, parts, outer_params, momentum, fragment)


def exchange(rows, experts):
    width = rows.shape[1]
    return lax.all_to_all(
        rows.reshape(experts, CAP, width), "chip", split_axis=0, concat_axis=0, tiled=True
    ).reshape(experts * CAP, width)


def shards(
    tokens,
    expert_ids,
    route_weights,
    w_gate,
    w_up,
    w_down,
    pseudo_values,
    block_scales,
    outer_params,
    momentum,
    fragment,
):
    experts = lax.axis_size("chip")
    buffer, combine = route(tokens, expert_ids, route_weights, experts)
    mine = exchange(buffer, experts)
    own = (w_gate, w_up, w_down)
    near, far = place_on("z_near"), place_on("z_far")
    parts = scatter_stage(dequant(near, pseudo_values, block_scales), "z_near")
    parts = scatter_stage(add_split(far, parts), "z_far")
    other = [shift(w, "core", 1) for w in own]
    part = add_parts(parts)
    mine, part = lax.optimization_barrier((mine, part))
    rows = expert_rows(mine, own, other)
    rows, apart = lax.optimization_barrier((rows, shift(part, "y_far", 1)))
    part = add_parts([part, apart])
    returned = exchange(rows, experts)
    moe_out = combine_rows(combine, returned)
    new_params, new_momentum = outer_step(part, outer_params, momentum, fragment)
    return (moe_out, new_params, new_momentum)


def solution(mesh):
    reps, exps = mesh.devices.shape
    fine = Mesh(
        mesh.devices.reshape(reps // (RADIX * RADIX), RADIX, RADIX, exps // 2, 2),
        ("y_far", "z_far", "z_near", "chip", "core"),
    )
    rep = ("y_far", "z_far", "z_near")
    exp = ("chip", "core")
    return jax.shard_map(
        shards,
        mesh=fine,
        in_specs=(
            P(rep + exp, None),
            P(rep + exp, None),
            P(rep + exp, None),
            P(exp, None, None),
            P(exp, None, None),
            P(exp, None, None),
            P(rep, exp, None),
            P(rep, exp, None),
            P(None, exp, None),
            P(exp, None),
            P(),
        ),
        out_specs=(P(rep + exp, None), P(exp, None), P(exp, None)),
        check_vma=False,
    )
```

```python
import functools

import jax
import jax.numpy as jnp
from jax import lax
from jax.experimental import pallas as pl
from jax.experimental.pallas import tpu as pltpu
from jax.sharding import Mesh
from jax.sharding import PartitionSpec as P

CAP = 16
RADIX = 4

momentum_rate = 0.9
outer_rate = 0.7

PARAMS = pltpu.CompilerParams(vmem_limit_bytes=20 * 1024 * 1024)
VMEM = pl.BlockSpec(memory_space=pltpu.VMEM)
HBM = pl.BlockSpec(memory_space=pltpu.HBM)
SMEM = pl.BlockSpec(memory_space=pltpu.SMEM)


def route_kernel(experts, ids_ref, weights_ref, tokens_ref, buffer_ref, combine_ref):
    topk, rows = ids_ref.shape
    ids = ids_ref[...]
    weights = weights_ref[...]
    expert = lax.broadcasted_iota(jnp.int32, (experts, rows), 0)
    named = jnp.zeros((experts, rows), jnp.float32)
    weight = jnp.zeros((experts, rows), jnp.float32)
    for k in range(topk):
        hit = ids[k : k + 1, :] == expert
        named = named + hit.astype(jnp.float32)
        weight = weight + jnp.where(hit, weights[k : k + 1, :], 0.0)
    earlier = lax.broadcasted_iota(jnp.int32, (rows, rows), 0) < lax.broadcasted_iota(
        jnp.int32, (rows, rows), 1
    )
    rank = jnp.dot(
        named.astype(jnp.bfloat16),
        earlier.astype(jnp.bfloat16),
        preferred_element_type=jnp.float32,
    ).astype(jnp.int32)
    rank = jnp.where(named > 0.5, rank, CAP)
    place = lax.broadcasted_iota(jnp.int32, (experts, CAP, rows), 1)
    chosen = rank[:, None, :] == place
    pick = jnp.where(chosen, 1.0, 0.0).reshape(experts * CAP, rows)
    combine_ref[...] = (
        jnp.where(chosen, jnp.broadcast_to(weight[:, None, :], chosen.shape), 0.0)
        .reshape(experts * CAP, rows)
        .astype(jnp.bfloat16)
    )
    buffer_ref[...] = jnp.dot(
        pick.astype(jnp.bfloat16), tokens_ref[...], preferred_element_type=jnp.float32
    ).astype(jnp.bfloat16)


def route(tokens, expert_ids, route_weights, experts):
    rows, width = tokens.shape
    return pl.pallas_call(
        functools.partial(route_kernel, experts),
        out_shape=(
            jax.ShapeDtypeStruct((experts * CAP, width), jnp.bfloat16),
            jax.ShapeDtypeStruct((experts * CAP, rows), jnp.bfloat16),
        ),
        compiler_params=PARAMS,
        name="route",
    )(expert_ids.T, route_weights.T, tokens)


def expert_kernel(rows_ref, gate_ref, up_ref, down_ref, *refs):
    sources, out_ref, targets, sems = refs[:3], refs[3], refs[4:7], refs[7]
    fetches = [
        pltpu.make_async_copy(source, target, sems.at[i])
        for i, (source, target) in enumerate(zip(sources, targets))
    ]
    for fetch in fetches:
        fetch.start()
    rows = rows_ref[...]

    def part(gate_ref, up_ref, down_ref, waits):
        for wait in waits[:1]:
            wait.wait()
        gate = jnp.dot(rows, gate_ref[0], preferred_element_type=jnp.float32)
        for wait in waits[1:2]:
            wait.wait()
        up = jnp.dot(rows, up_ref[0], preferred_element_type=jnp.float32)
        hidden = (gate / (1.0 + jnp.exp(-gate)) * up).astype(jnp.bfloat16)
        for wait in waits[2:]:
            wait.wait()
        return jnp.dot(hidden, down_ref[0], preferred_element_type=jnp.float32)

    total = part(gate_ref, up_ref, down_ref, []) + part(*targets, fetches)
    out_ref[...] = total.astype(jnp.bfloat16)


def expert_rows(rows, own, other):
    return pl.pallas_call(
        expert_kernel,
        in_specs=[VMEM] * 4 + [HBM] * 3,
        out_shape=jax.ShapeDtypeStruct(rows.shape, jnp.bfloat16),
        scratch_shapes=[pltpu.VMEM(x.shape, x.dtype) for x in other]
        + [pltpu.SemaphoreType.DMA((3,))],
        compiler_params=PARAMS,
        name="expert_rows",
    )(rows, *own, *other)


def combine_kernel(combine_ref, rows_ref, out_ref):
    out_ref[...] = lax.dot_general(
        combine_ref[...],
        rows_ref[...],
        (((0,), (0,)), ((), ())),
        preferred_element_type=jnp.float32,
    ).astype(jnp.bfloat16)


def combine_rows(combine, rows):
    return pl.pallas_call(
        combine_kernel,
        out_shape=jax.ShapeDtypeStruct((combine.shape[1], rows.shape[1]), jnp.bfloat16),
        compiler_params=PARAMS,
        name="combine_rows",
    )(combine, rows)


def dequant_kernel(z_ref, values_ref, scales_ref, *out_refs):
    rows, width = out_refs[0].shape
    blocks = scales_ref.shape[0]
    column = lax.broadcasted_iota(jnp.int32, (blocks, width), 1) // (width // blocks)
    spread = (column == lax.broadcasted_iota(jnp.int32, (blocks, width), 0)).astype(jnp.bfloat16)
    scales = scales_ref[...]
    high = scales.astype(jnp.bfloat16)
    rest = scales - high.astype(jnp.float32)
    middle = rest.astype(jnp.bfloat16)
    low = (rest - middle.astype(jnp.float32)).astype(jnp.bfloat16)
    wide = sum(
        lax.dot_general(
            part, spread, (((0,), (0,)), ((), ())), preferred_element_type=jnp.float32
        )
        for part in (high, middle, low)
    )
    whole = (values_ref[0].astype(jnp.float32) * wide).astype(jnp.bfloat16)
    for place in range(RADIX):
        block = whole[place * rows : (place + 1) * rows]
        for step, out_ref in enumerate(out_refs):

            @pl.when((z_ref[0] + step) % RADIX == place)
            def _():
                out_ref[...] = block


def dequant(z, values, scales):
    _, rows, width = values.shape
    part = jax.ShapeDtypeStruct((rows // RADIX, width), jnp.bfloat16)
    return pl.pallas_call(
        dequant_kernel,
        in_specs=[SMEM, VMEM, VMEM],
        out_shape=(part,) * RADIX,
        compiler_params=PARAMS,
        name="dequant",
    )(z, values, scales[0].T)


def add_split_kernel(z_ref, *refs):
    in_refs, out_refs = refs[:RADIX], refs[RADIX:]
    total = sum(ref[...].astype(jnp.float32) for ref in in_refs).astype(jnp.bfloat16)
    width = out_refs[0].shape[1]
    for place in range(RADIX):
        for step, out_ref in enumerate(out_refs):

            @pl.when((z_ref[0] // RADIX + step) % RADIX == place)
            def _():
                out_ref[...] = total[:, place * width : (place + 1) * width]


def add_split(z, parts):
    rows, width = parts[0].shape
    part = jax.ShapeDtypeStruct((rows, width // RADIX), jnp.bfloat16)
    return pl.pallas_call(
        add_split_kernel,
        in_specs=[SMEM] + [VMEM] * RADIX,
        out_shape=(part,) * RADIX,
        compiler_params=PARAMS,
        name="add_split",
    )(z, *parts)


def add_kernel(*refs):
    refs[-1][...] = sum(ref[...].astype(jnp.float32) for ref in refs[:-1]).astype(jnp.bfloat16)


def add_parts(parts):
    return pl.pallas_call(
        add_kernel,
        out_shape=jax.ShapeDtypeStruct(parts[0].shape, jnp.bfloat16),
        compiler_params=PARAMS,
        name="add_parts",
    )(*parts)


def total_kernel(one_ref, other_ref, out_ref):
    total = (one_ref[...].astype(jnp.float32) + other_ref[...].astype(jnp.float32)).astype(
        jnp.bfloat16
    )
    out_ref[...] = jnp.broadcast_to(total[None], out_ref.shape)


def total_spread(one, other, copies):
    return pl.pallas_call(
        total_kernel,
        out_shape=jax.ShapeDtypeStruct((copies,) + one.shape, jnp.bfloat16),
        compiler_params=PARAMS,
        name="total_spread",
    )(one, other)


def update_kernel(replicas, fragment_ref, totals_ref, base_ref, momentum_ref, params_out, momentum_out):
    pieces, rows, span = totals_ref.shape
    for piece in range(pieces):
        far, near = piece // RADIX, piece % RADIX
        at = (pl.ds(near * rows, rows), pl.ds(far * span, span))
        delta = totals_ref[piece].astype(jnp.float32) / replicas
        new_momentum = momentum_rate * momentum_ref[at] + delta
        momentum_out[at] = new_momentum
        params_out[at] = base_ref[(0,) + at] - outer_rate * (delta + momentum_rate * new_momentum)


def update(replicas, totals, outer_params, momentum, fragment):
    shape = momentum.shape

    def whole(block):
        return pl.BlockSpec(block, lambda i, fragment_ref: (0,) * len(block))

    return pl.pallas_call(
        functools.partial(update_kernel, replicas),
        grid_spec=pltpu.PrefetchScalarGridSpec(
            num_scalar_prefetch=1,
            grid=(1,),
            in_specs=[
                whole(totals.shape),
                pl.BlockSpec((1,) + shape, lambda i, fragment_ref: (fragment_ref[0], 0, 0)),
                whole(shape),
            ],
            out_specs=(whole(shape), whole(shape)),
        ),
        out_shape=(
            jax.ShapeDtypeStruct(shape, jnp.float32),
            jax.ShapeDtypeStruct(shape, jnp.float32),
        ),
        compiler_params=PARAMS,
        name="update",
    )(fragment, totals, outer_params, momentum)


def shift(part, axis, step):
    size = lax.axis_size(axis)
    return lax.ppermute(part, axis, [(i, (i + step) % size) for i in range(size)])


def near_shift(part, step):
    def target(i):
        return i // RADIX * RADIX + (i + step) % RADIX

    return lax.ppermute(part, "z", [(i, target(i)) for i in range(lax.axis_size("z"))])


def far_shift(part, step):
    return shift(part, "z", RADIX * step)


def scatter_stage(parts, move):
    return [parts[0]] + [move(parts[step], step) for step in range(1, RADIX)]


def gather_z(parts):
    return lax.all_to_all(parts, "z", split_axis=0, concat_axis=0, tiled=True)


def exchange(rows, experts):
    width = rows.shape[1]
    return lax.all_to_all(
        rows.reshape(experts, CAP, width), "chip", split_axis=0, concat_axis=0, tiled=True
    ).reshape(experts * CAP, width)


def shards(
    tokens,
    expert_ids,
    route_weights,
    w_gate,
    w_up,
    w_down,
    pseudo_values,
    block_scales,
    outer_params,
    momentum,
    fragment,
):
    experts = lax.axis_size("chip")
    buffer, combine = route(tokens, expert_ids, route_weights, experts)
    mine = exchange(buffer, experts)
    own = (w_gate, w_up, w_down)
    z = lax.axis_index("z").astype(jnp.int32).reshape(1)
    parts = scatter_stage(dequant(z, pseudo_values, block_scales), near_shift)
    parts = add_split(z, parts)
    other = [shift(w, "core", 1) for w in own]
    mine, parts = lax.optimization_barrier((mine, parts))
    rows = expert_rows(mine, own, other)
    rows, parts = lax.optimization_barrier((rows, parts))
    returned = exchange(rows, experts)
    part = add_parts(scatter_stage(parts, far_shift))
    returned, part = lax.optimization_barrier((returned, part))
    spread = total_spread(part, shift(part, "y_far", 1), lax.axis_size("z"))
    moe_out = combine_rows(combine, returned)
    new_params, new_momentum = update(
        lax.axis_size(("y_far", "z")), gather_z(spread), outer_params, momentum, fragment
    )
    return (moe_out, new_params, new_momentum)


def solution(mesh):
    reps, exps = mesh.devices.shape
    fine = Mesh(
        mesh.devices.reshape(reps // (RADIX * RADIX), RADIX * RADIX, exps // 2, 2),
        ("y_far", "z", "chip", "core"),
    )
    rep = ("y_far", "z")
    exp = ("chip", "core")
    return jax.shard_map(
        shards,
        mesh=fine,
        in_specs=(
            P(rep + exp, None),
            P(rep + exp, None),
            P(rep + exp, None),
            P(exp, None, None),
            P(exp, None, None),
            P(exp, None, None),
            P(rep, exp, None),
            P(rep, exp, None),
            P(None, exp, None),
            P(exp, None),
            P(),
        ),
        out_specs=(P(rep + exp, None), P(exp, None), P(exp, None)),
        check_vma=False,
    )
```

```python
import functools

import jax
import jax.numpy as jnp
from jax import lax
from jax.experimental import pallas as pl
from jax.experimental.pallas import tpu as pltpu
from jax.sharding import Mesh
from jax.sharding import PartitionSpec as P

CAP = 16
RADIX = 4

momentum_rate = 0.9
outer_rate = 0.7

PARAMS = pltpu.CompilerParams(vmem_limit_bytes=20 * 1024 * 1024)
VMEM = pl.BlockSpec(memory_space=pltpu.VMEM)
HBM = pl.BlockSpec(memory_space=pltpu.HBM)
SMEM = pl.BlockSpec(memory_space=pltpu.SMEM)


def route_kernel(experts, ids_ref, weights_ref, tokens_ref, buffer_ref, combine_ref):
    topk, rows = ids_ref.shape
    ids = ids_ref[...]
    weights = weights_ref[...]
    expert = lax.broadcasted_iota(jnp.int32, (experts, rows), 0)
    named = jnp.zeros((experts, rows), jnp.float32)
    weight = jnp.zeros((experts, rows), jnp.float32)
    for k in range(topk):
        hit = ids[k : k + 1, :] == expert
        named = named + hit.astype(jnp.float32)
        weight = weight + jnp.where(hit, weights[k : k + 1, :], 0.0)
    earlier = lax.broadcasted_iota(jnp.int32, (rows, rows), 0) < lax.broadcasted_iota(
        jnp.int32, (rows, rows), 1
    )
    rank = jnp.dot(
        named.astype(jnp.bfloat16),
        earlier.astype(jnp.bfloat16),
        preferred_element_type=jnp.float32,
    ).astype(jnp.int32)
    rank = jnp.where(named > 0.5, rank, CAP)
    place = lax.broadcasted_iota(jnp.int32, (experts, CAP, rows), 1)
    chosen = rank[:, None, :] == place
    pick = jnp.where(chosen, 1.0, 0.0).reshape(experts * CAP, rows)
    combine_ref[...] = (
        jnp.where(chosen, jnp.broadcast_to(weight[:, None, :], chosen.shape), 0.0)
        .reshape(experts * CAP, rows)
        .astype(jnp.bfloat16)
    )
    buffer_ref[...] = jnp.dot(
        pick.astype(jnp.bfloat16), tokens_ref[...], preferred_element_type=jnp.float32
    ).astype(jnp.bfloat16)


def route(tokens, expert_ids, route_weights, experts):
    rows, width = tokens.shape
    return pl.pallas_call(
        functools.partial(route_kernel, experts),
        out_shape=(
            jax.ShapeDtypeStruct((experts * CAP, width), jnp.bfloat16),
            jax.ShapeDtypeStruct((experts * CAP, rows), jnp.bfloat16),
        ),
        compiler_params=PARAMS,
        name="route",
    )(expert_ids.T, route_weights.T, tokens)


def expert_kernel(rows_ref, gate_ref, up_ref, down_ref, *refs):
    sources, out_ref, targets, sems = refs[:3], refs[3], refs[4:7], refs[7]
    fetches = [
        pltpu.make_async_copy(source, target, sems.at[i])
        for i, (source, target) in enumerate(zip(sources, targets))
    ]
    for fetch in fetches:
        fetch.start()
    rows = rows_ref[...]

    def part(gate_ref, up_ref, down_ref, waits):
        for wait in waits[:1]:
            wait.wait()
        gate = jnp.dot(rows, gate_ref[0], preferred_element_type=jnp.float32)
        for wait in waits[1:2]:
            wait.wait()
        up = jnp.dot(rows, up_ref[0], preferred_element_type=jnp.float32)
        hidden = (gate / (1.0 + jnp.exp(-gate)) * up).astype(jnp.bfloat16)
        for wait in waits[2:]:
            wait.wait()
        return jnp.dot(hidden, down_ref[0], preferred_element_type=jnp.float32)

    total = part(gate_ref, up_ref, down_ref, []) + part(*targets, fetches)
    out_ref[...] = total.astype(jnp.bfloat16)


def expert_rows(rows, own, other):
    return pl.pallas_call(
        expert_kernel,
        in_specs=[VMEM] * 4 + [HBM] * 3,
        out_shape=jax.ShapeDtypeStruct(rows.shape, jnp.bfloat16),
        scratch_shapes=[pltpu.VMEM(x.shape, x.dtype) for x in other]
        + [pltpu.SemaphoreType.DMA((3,))],
        compiler_params=PARAMS,
        name="expert_rows",
    )(rows, *own, *other)


def combine_kernel(combine_ref, rows_ref, out_ref):
    out_ref[...] = lax.dot_general(
        combine_ref[...],
        rows_ref[...],
        (((0,), (0,)), ((), ())),
        preferred_element_type=jnp.float32,
    ).astype(jnp.bfloat16)


def combine_rows(combine, rows):
    return pl.pallas_call(
        combine_kernel,
        out_shape=jax.ShapeDtypeStruct((combine.shape[1], rows.shape[1]), jnp.bfloat16),
        compiler_params=PARAMS,
        name="combine_rows",
    )(combine, rows)


def dequant_kernel(place_ref, values_ref, scales_ref, *out_refs):
    rows, width = out_refs[0].shape
    blocks = scales_ref.shape[0]
    column = lax.broadcasted_iota(jnp.int32, (blocks, width), 1) // (width // blocks)
    spread = (column == lax.broadcasted_iota(jnp.int32, (blocks, width), 0)).astype(jnp.bfloat16)
    scales = scales_ref[...]
    high = scales.astype(jnp.bfloat16)
    rest = scales - high.astype(jnp.float32)
    middle = rest.astype(jnp.bfloat16)
    low = (rest - middle.astype(jnp.float32)).astype(jnp.bfloat16)
    wide = sum(
        lax.dot_general(
            part, spread, (((0,), (0,)), ((), ())), preferred_element_type=jnp.float32
        )
        for part in (high, middle, low)
    )
    whole = (values_ref[0].astype(jnp.float32) * wide).astype(jnp.bfloat16)
    for place in range(RADIX):
        block = whole[place * rows : (place + 1) * rows]
        for step, out_ref in enumerate(out_refs):

            @pl.when((place_ref[0] + step) % RADIX == place)
            def _():
                out_ref[...] = block


def dequant(place, values, scales):
    _, rows, width = values.shape
    part = jax.ShapeDtypeStruct((rows // RADIX, width), jnp.bfloat16)
    return pl.pallas_call(
        dequant_kernel,
        in_specs=[SMEM, VMEM, VMEM],
        out_shape=(part,) * RADIX,
        compiler_params=PARAMS,
        name="dequant",
    )(place, values, scales[0].T)


def add_kernel(*refs):
    refs[-1][...] = sum(ref[...].astype(jnp.float32) for ref in refs[:-1]).astype(jnp.bfloat16)


def add_parts(parts):
    return pl.pallas_call(
        add_kernel,
        out_shape=jax.ShapeDtypeStruct(parts[0].shape, jnp.bfloat16),
        compiler_params=PARAMS,
        name="add_parts",
    )(*parts)


def total_kernel(parts_ref, out_ref):
    total = jnp.sum(parts_ref[...].astype(jnp.float32), axis=0).astype(jnp.bfloat16)
    out_ref[...] = jnp.broadcast_to(total[None], out_ref.shape)


def total_spread(parts):
    return pl.pallas_call(
        total_kernel,
        out_shape=jax.ShapeDtypeStruct((RADIX,) + parts.shape[1:], jnp.bfloat16),
        compiler_params=PARAMS,
        name="total_spread",
    )(parts)


def update_kernel(replicas, fragment_ref, totals_ref, base_ref, momentum_ref, params_out, momentum_out):
    pieces, rows, _ = totals_ref.shape
    for piece in range(pieces):
        at = pl.ds(piece * rows, rows)
        delta = totals_ref[piece].astype(jnp.float32) / replicas
        new_momentum = momentum_rate * momentum_ref[at, :] + delta
        momentum_out[at, :] = new_momentum
        params_out[at, :] = base_ref[0, at, :] - outer_rate * (
            delta + momentum_rate * new_momentum
        )


def update(replicas, totals, outer_params, momentum, fragment):
    shape = momentum.shape

    def whole(block):
        return pl.BlockSpec(block, lambda i, fragment_ref: (0,) * len(block))

    return pl.pallas_call(
        functools.partial(update_kernel, replicas),
        grid_spec=pltpu.PrefetchScalarGridSpec(
            num_scalar_prefetch=1,
            grid=(1,),
            in_specs=[
                whole(totals.shape),
                pl.BlockSpec((1,) + shape, lambda i, fragment_ref: (fragment_ref[0], 0, 0)),
                whole(shape),
            ],
            out_specs=(whole(shape), whole(shape)),
        ),
        out_shape=(
            jax.ShapeDtypeStruct(shape, jnp.float32),
            jax.ShapeDtypeStruct(shape, jnp.float32),
        ),
        compiler_params=PARAMS,
        name="update",
    )(fragment, totals, outer_params, momentum)


def shift(part, axis, step):
    size = lax.axis_size(axis)
    return lax.ppermute(part, axis, [(i, (i + step) % size) for i in range(size)])


def scatter_stage(parts, axis):
    return [parts[0]] + [shift(parts[step], axis, step) for step in range(1, RADIX)]


def place_on(axis):
    return lax.axis_index(axis).astype(jnp.int32).reshape(1)


def exchange(rows, experts):
    width = rows.shape[1]
    return lax.all_to_all(
        rows.reshape(experts, CAP, width), "chip", split_axis=0, concat_axis=0, tiled=True
    ).reshape(experts * CAP, width)


def shards(
    tokens,
    expert_ids,
    route_weights,
    w_gate,
    w_up,
    w_down,
    pseudo_values,
    block_scales,
    outer_params,
    momentum,
    fragment,
):
    experts = lax.axis_size("chip")
    buffer, combine = route(tokens, expert_ids, route_weights, experts)
    mine = exchange(buffer, experts)
    own = (w_gate, w_up, w_down)
    near = place_on("z_near")
    part = add_parts(scatter_stage(dequant(near, pseudo_values, block_scales), "z_near"))
    other = [shift(w, "core", 1) for w in own]
    mine, part = lax.optimization_barrier((mine, part))
    rows = expert_rows(mine, own, other)
    rows, apart = lax.optimization_barrier((rows, shift(part, "y_far", 1)))
    part = add_parts([part, apart])
    returned = exchange(rows, experts)
    spread = total_spread(lax.all_gather(part, "z_far", axis=0))
    returned, spread = lax.optimization_barrier((returned, spread))
    totals = lax.all_to_all(spread, "z_near", split_axis=0, concat_axis=0, tiled=True)
    moe_out = combine_rows(combine, returned)
    new_params, new_momentum = update(
        lax.axis_size(("y_far", "z_far", "z_near")), totals, outer_params, momentum, fragment
    )
    return (moe_out, new_params, new_momentum)


def solution(mesh):
    reps, exps = mesh.devices.shape
    fine = Mesh(
        mesh.devices.reshape(reps // (RADIX * RADIX), RADIX, RADIX, exps // 2, 2),
        ("y_far", "z_far", "z_near", "chip", "core"),
    )
    rep = ("y_far", "z_far", "z_near")
    exp = ("chip", "core")
    return jax.shard_map(
        shards,
        mesh=fine,
        in_specs=(
            P(rep + exp, None),
            P(rep + exp, None),
            P(rep + exp, None),
            P(exp, None, None),
            P(exp, None, None),
            P(exp, None, None),
            P(rep, exp, None),
            P(rep, exp, None),
            P(None, exp, None),
            P(exp, None),
            P(),
        ),
        out_specs=(P(rep + exp, None), P(exp, None), P(exp, None)),
        check_vma=False,
    )
```

```python
import functools

import jax
import jax.numpy as jnp
from jax import lax
from jax.experimental import pallas as pl
from jax.experimental.pallas import tpu as pltpu
from jax.sharding import Mesh
from jax.sharding import PartitionSpec as P

CAP = 16
RADIX = 4

momentum_rate = 0.9
outer_rate = 0.7

ROUTE_PARAMS = pltpu.CompilerParams(vmem_limit_bytes=62 * 1024 * 1024)
EXPERT_PARAMS = pltpu.CompilerParams(vmem_limit_bytes=62 * 1024 * 1024)
PARAMS = pltpu.CompilerParams(vmem_limit_bytes=20 * 1024 * 1024)
VMEM = pl.BlockSpec(memory_space=pltpu.VMEM)
HBM = pl.BlockSpec(memory_space=pltpu.HBM)
SMEM = pl.BlockSpec(memory_space=pltpu.SMEM)


def route_kernel(experts, *refs):
    sources, (buffer_ref, combine_ref), targets, sems = refs[:3], refs[3:5], refs[5:8], refs[8]
    fetches = [
        pltpu.make_async_copy(source, target, sems.at[i])
        for i, (source, target) in enumerate(zip(sources, targets))
    ]
    for fetch in fetches:
        fetch.start()
    ids_ref, weights_ref, tokens_ref = targets
    topk, rows = ids_ref.shape
    fetches[0].wait()
    ids = ids_ref[...]
    fetches[1].wait()
    weights = weights_ref[...]
    expert = lax.broadcasted_iota(jnp.int32, (experts, rows), 0)
    named = jnp.zeros((experts, rows), jnp.float32)
    weight = jnp.zeros((experts, rows), jnp.float32)
    for k in range(topk):
        hit = ids[k : k + 1, :] == expert
        named = named + hit.astype(jnp.float32)
        weight = weight + jnp.where(hit, weights[k : k + 1, :], 0.0)
    earlier = lax.broadcasted_iota(jnp.int32, (rows, rows), 0) < lax.broadcasted_iota(
        jnp.int32, (rows, rows), 1
    )
    rank = jnp.dot(
        named.astype(jnp.bfloat16),
        earlier.astype(jnp.bfloat16),
        preferred_element_type=jnp.float32,
    ).astype(jnp.int32)
    rank = jnp.where(named > 0.5, rank, CAP)
    place = lax.broadcasted_iota(jnp.int32, (experts, CAP, rows), 1)
    chosen = rank[:, None, :] == place
    pick = jnp.where(chosen, 1.0, 0.0).reshape(experts * CAP, rows)
    combine_ref[...] = (
        jnp.where(chosen, jnp.broadcast_to(weight[:, None, :], chosen.shape), 0.0)
        .reshape(experts * CAP, rows)
        .astype(jnp.bfloat16)
    )
    fetches[2].wait()
    buffer_ref[...] = jnp.dot(
        pick.astype(jnp.bfloat16), tokens_ref[...], preferred_element_type=jnp.float32
    ).astype(jnp.bfloat16)


def route(tokens, expert_ids, route_weights, experts):
    rows, width = tokens.shape
    operands = (expert_ids.T, route_weights.T, tokens)
    return pl.pallas_call(
        functools.partial(route_kernel, experts),
        out_shape=(
            jax.ShapeDtypeStruct((experts * CAP, width), jnp.bfloat16),
            jax.ShapeDtypeStruct((experts * CAP, rows), jnp.bfloat16),
        ),
        in_specs=[HBM] * len(operands),
        scratch_shapes=[pltpu.VMEM(x.shape, x.dtype) for x in operands]
        + [pltpu.SemaphoreType.DMA((len(operands),))],
        compiler_params=ROUTE_PARAMS,
        name="route",
    )(*operands)


def expert_kernel(rows_ref, *refs):
    sources, out_ref, targets, sems = refs[:6], refs[6], refs[7:13], refs[13]
    fetches = [
        pltpu.make_async_copy(source, target, sems.at[i])
        for i, (source, target) in enumerate(zip(sources, targets))
    ]
    for fetch in fetches:
        fetch.start()
    rows = rows_ref[...]
    total = None
    for first in (0, 3):
        fetches[first].wait()
        gate = jnp.dot(rows, targets[first][0], preferred_element_type=jnp.float32)
        fetches[first + 1].wait()
        up = jnp.dot(rows, targets[first + 1][0], preferred_element_type=jnp.float32)
        hidden = (gate / (1.0 + jnp.exp(-gate)) * up).astype(jnp.bfloat16)
        fetches[first + 2].wait()
        part = jnp.dot(hidden, targets[first + 2][0], preferred_element_type=jnp.float32)
        total = part if total is None else total + part
    out_ref[...] = total.astype(jnp.bfloat16)


def expert_rows(rows, own, other):
    weights = own + other
    return pl.pallas_call(
        expert_kernel,
        in_specs=[VMEM] + [HBM] * len(weights),
        out_shape=jax.ShapeDtypeStruct(rows.shape, jnp.bfloat16),
        scratch_shapes=[pltpu.VMEM(x.shape, x.dtype) for x in weights]
        + [pltpu.SemaphoreType.DMA((len(weights),))],
        compiler_params=EXPERT_PARAMS,
        name="expert_rows",
    )(rows, *weights)


def combine_kernel(combine_ref, rows_ref, out_ref):
    out_ref[...] = lax.dot_general(
        combine_ref[...],
        rows_ref[...],
        (((0,), (0,)), ((), ())),
        preferred_element_type=jnp.float32,
    ).astype(jnp.bfloat16)


def combine_rows(combine, rows):
    return pl.pallas_call(
        combine_kernel,
        out_shape=jax.ShapeDtypeStruct((combine.shape[1], rows.shape[1]), jnp.bfloat16),
        compiler_params=PARAMS,
        name="combine_rows",
    )(combine, rows)


def dequant_kernel(place_ref, values_ref, scales_ref, *out_refs):
    rows, width = out_refs[0].shape
    blocks = scales_ref.shape[0]
    column = lax.broadcasted_iota(jnp.int32, (blocks, width), 1) // (width // blocks)
    spread = (column == lax.broadcasted_iota(jnp.int32, (blocks, width), 0)).astype(jnp.bfloat16)
    scales = scales_ref[...]
    high = scales.astype(jnp.bfloat16)
    rest = scales - high.astype(jnp.float32)
    middle = rest.astype(jnp.bfloat16)
    low = (rest - middle.astype(jnp.float32)).astype(jnp.bfloat16)
    wide = sum(
        lax.dot_general(
            part, spread, (((0,), (0,)), ((), ())), preferred_element_type=jnp.float32
        )
        for part in (high, middle, low)
    )
    whole = (values_ref[0].astype(jnp.float32) * wide).astype(jnp.bfloat16)
    for place in range(RADIX):
        block = whole[place * rows : (place + 1) * rows]
        for step, out_ref in enumerate(out_refs):

            @pl.when((place_ref[0] + step) % RADIX == place)
            def _():
                out_ref[...] = block


def dequant(place, values, scales):
    _, rows, width = values.shape
    part = jax.ShapeDtypeStruct((rows // RADIX, width), jnp.bfloat16)
    return pl.pallas_call(
        dequant_kernel,
        in_specs=[SMEM, VMEM, VMEM],
        out_shape=(part,) * RADIX,
        compiler_params=PARAMS,
        name="dequant",
    )(place, values, scales[0].T)


def add_kernel(*refs):
    refs[-1][...] = sum(ref[...].astype(jnp.float32) for ref in refs[:-1]).astype(jnp.bfloat16)


def add_parts(parts):
    return pl.pallas_call(
        add_kernel,
        out_shape=jax.ShapeDtypeStruct(parts[0].shape, jnp.bfloat16),
        compiler_params=PARAMS,
        name="add_parts",
    )(*parts)


def total_kernel(parts_ref, out_ref):
    total = jnp.sum(parts_ref[...].astype(jnp.float32), axis=0).astype(jnp.bfloat16)
    out_ref[...] = jnp.broadcast_to(total[None], out_ref.shape)


def total_spread(parts):
    return pl.pallas_call(
        total_kernel,
        out_shape=jax.ShapeDtypeStruct((RADIX,) + parts.shape[1:], jnp.bfloat16),
        compiler_params=PARAMS,
        name="total_spread",
    )(parts)


def update_kernel(replicas, fragment_ref, totals_ref, base_ref, momentum_ref, params_out, momentum_out):
    pieces, rows, _ = totals_ref.shape
    for piece in range(pieces):
        at = pl.ds(piece * rows, rows)
        delta = totals_ref[piece].astype(jnp.float32) / replicas
        new_momentum = momentum_rate * momentum_ref[at, :] + delta
        momentum_out[at, :] = new_momentum
        params_out[at, :] = base_ref[0, at, :] - outer_rate * (
            delta + momentum_rate * new_momentum
        )


def update(replicas, totals, outer_params, momentum, fragment):
    shape = momentum.shape

    def whole(block):
        return pl.BlockSpec(block, lambda i, fragment_ref: (0,) * len(block))

    return pl.pallas_call(
        functools.partial(update_kernel, replicas),
        grid_spec=pltpu.PrefetchScalarGridSpec(
            num_scalar_prefetch=1,
            grid=(1,),
            in_specs=[
                whole(totals.shape),
                pl.BlockSpec((1,) + shape, lambda i, fragment_ref: (fragment_ref[0], 0, 0)),
                whole(shape),
            ],
            out_specs=(whole(shape), whole(shape)),
        ),
        out_shape=(
            jax.ShapeDtypeStruct(shape, jnp.float32),
            jax.ShapeDtypeStruct(shape, jnp.float32),
        ),
        compiler_params=PARAMS,
        name="update",
    )(fragment, totals, outer_params, momentum)


def shift(part, axis, step):
    size = lax.axis_size(axis)
    return lax.ppermute(part, axis, [(i, (i + step) % size) for i in range(size)])


def scatter_stage(parts, axis):
    return [parts[0]] + [shift(parts[step], axis, step) for step in range(1, RADIX)]


def place_on(axis):
    return lax.axis_index(axis).astype(jnp.int32).reshape(1)


def exchange(rows, experts):
    width = rows.shape[1]
    return lax.all_to_all(
        rows.reshape(experts, CAP, width), "chip", split_axis=0, concat_axis=0, tiled=True
    ).reshape(experts * CAP, width)


def shards(
    tokens,
    expert_ids,
    route_weights,
    w_gate,
    w_up,
    w_down,
    pseudo_values,
    block_scales,
    outer_params,
    momentum,
    fragment,
):
    experts = lax.axis_size("chip")
    buffer, combine = route(tokens, expert_ids, route_weights, experts)
    mine = exchange(buffer, experts)
    own = (w_gate, w_up, w_down)
    near = place_on("z_near")
    part = add_parts(scatter_stage(dequant(near, pseudo_values, block_scales), "z_near"))
    apart = shift(part, "y_far", 1)
    other = tuple(shift(w, "core", 1) for w in own)
    mine, part = lax.optimization_barrier((mine, part))
    rows = expert_rows(mine, own, other)
    rows, apart = lax.optimization_barrier((rows, apart))
    part = add_parts([part, apart])
    returned = exchange(rows, experts)
    spread = total_spread(lax.all_gather(part, "z_far", axis=0))
    returned, spread = lax.optimization_barrier((returned, spread))
    totals = lax.all_to_all(spread, "z_near", split_axis=0, concat_axis=0, tiled=True)
    moe_out = combine_rows(combine, returned)
    new_params, new_momentum = update(
        lax.axis_size(("y_far", "z_far", "z_near")), totals, outer_params, momentum, fragment
    )
    return (moe_out, new_params, new_momentum)


def solution(mesh):
    reps, exps = mesh.devices.shape
    fine = Mesh(
        mesh.devices.reshape(reps // (RADIX * RADIX), RADIX, RADIX, exps // 2, 2),
        ("y_far", "z_far", "z_near", "chip", "core"),
    )
    rep = ("y_far", "z_far", "z_near")
    exp = ("chip", "core")
    return jax.shard_map(
        shards,
        mesh=fine,
        in_specs=(
            P(rep + exp, None),
            P(rep + exp, None),
            P(rep + exp, None),
            P(exp, None, None),
            P(exp, None, None),
            P(exp, None, None),
            P(rep, exp, None),
            P(rep, exp, None),
            P(None, exp, None),
            P(exp, None),
            P(),
        ),
        out_specs=(P(rep + exp, None), P(exp, None), P(exp, None)),
        check_vma=False,
    )
```

```python
import functools

import jax
import jax.numpy as jnp
from jax import lax
from jax.experimental import pallas as pl
from jax.experimental.pallas import tpu as pltpu
from jax.sharding import Mesh
from jax.sharding import PartitionSpec as P

CAP = 16
RADIX = 4

momentum_rate = 0.9
outer_rate = 0.7

ROUTE_PARAMS = pltpu.CompilerParams(vmem_limit_bytes=62 * 1024 * 1024)
EXPERT_PARAMS = pltpu.CompilerParams(vmem_limit_bytes=63 * 1024 * 1024)
PARAMS = pltpu.CompilerParams(vmem_limit_bytes=20 * 1024 * 1024)
VMEM = pl.BlockSpec(memory_space=pltpu.VMEM)
HBM = pl.BlockSpec(memory_space=pltpu.HBM)
SMEM = pl.BlockSpec(memory_space=pltpu.SMEM)


def route_kernel(experts, *refs):
    sources, (buffer_ref, combine_ref), targets, sems = refs[:3], refs[3:5], refs[5:8], refs[8]
    fetches = [
        pltpu.make_async_copy(source, target, sems.at[i])
        for i, (source, target) in enumerate(zip(sources, targets))
    ]
    for fetch in fetches:
        fetch.start()
    ids_ref, weights_ref, tokens_ref = targets
    topk, rows = ids_ref.shape
    fetches[0].wait()
    ids = ids_ref[...]
    fetches[1].wait()
    weights = weights_ref[...]
    expert = lax.broadcasted_iota(jnp.int32, (experts, rows), 0)
    named = jnp.zeros((experts, rows), jnp.float32)
    weight = jnp.zeros((experts, rows), jnp.float32)
    for k in range(topk):
        hit = ids[k : k + 1, :] == expert
        named = named + hit.astype(jnp.float32)
        weight = weight + jnp.where(hit, weights[k : k + 1, :], 0.0)
    earlier = lax.broadcasted_iota(jnp.int32, (rows, rows), 0) < lax.broadcasted_iota(
        jnp.int32, (rows, rows), 1
    )
    rank = jnp.dot(
        named.astype(jnp.bfloat16),
        earlier.astype(jnp.bfloat16),
        preferred_element_type=jnp.float32,
    ).astype(jnp.int32)
    rank = jnp.where(named > 0.5, rank, CAP)
    place = lax.broadcasted_iota(jnp.int32, (experts, CAP, rows), 1)
    chosen = rank[:, None, :] == place
    pick = jnp.where(chosen, 1.0, 0.0).reshape(experts * CAP, rows)
    combine_ref[...] = (
        jnp.where(chosen, jnp.broadcast_to(weight[:, None, :], chosen.shape), 0.0)
        .reshape(experts * CAP, rows)
        .astype(jnp.bfloat16)
    )
    fetches[2].wait()
    buffer_ref[...] = jnp.dot(
        pick.astype(jnp.bfloat16), tokens_ref[...], preferred_element_type=jnp.float32
    ).astype(jnp.bfloat16)


def route(tokens, expert_ids, route_weights, experts):
    rows, width = tokens.shape
    operands = (expert_ids.T, route_weights.T, tokens)
    return pl.pallas_call(
        functools.partial(route_kernel, experts),
        out_shape=(
            jax.ShapeDtypeStruct((experts * CAP, width), jnp.bfloat16),
            jax.ShapeDtypeStruct((experts * CAP, rows), jnp.bfloat16),
        ),
        in_specs=[HBM] * len(operands),
        scratch_shapes=[pltpu.VMEM(x.shape, x.dtype) for x in operands]
        + [pltpu.SemaphoreType.DMA((len(operands),))],
        compiler_params=ROUTE_PARAMS,
        name="route",
    )(*operands)


def expert_kernel(rows_hbm, *refs):
    sources, out_ref, targets, sems = refs[:6], refs[6], refs[7:11], refs[11]
    rows_ref, gate_ref, up_ref, down_ref = targets
    half = gate_ref.shape[1] // 2
    moves = [(rows_hbm, rows_ref)]
    for kind, target in enumerate((gate_ref, up_ref, down_ref)):
        for side in range(2):
            span = pl.ds(side * half, half)
            source = sources[3 * side + kind].at[0]
            moves.append((source, target.at[span] if kind == 2 else target.at[:, span]))
    fetches = [
        pltpu.make_async_copy(source, target, sems.at[i])
        for i, (source, target) in enumerate(moves)
    ]
    for fetch in fetches[:5]:
        fetch.start()
    for fetch in fetches[:3]:
        fetch.wait()
    for fetch in fetches[5:]:
        fetch.start()
    rows = rows_ref[...]
    gate = jnp.dot(rows, gate_ref[...], preferred_element_type=jnp.float32)
    for fetch in fetches[3:5]:
        fetch.wait()
    up = jnp.dot(rows, up_ref[...], preferred_element_type=jnp.float32)
    hidden = (gate / (1.0 + jnp.exp(-gate)) * up).astype(jnp.bfloat16)
    for fetch in fetches[5:]:
        fetch.wait()
    out_ref[...] = jnp.dot(hidden, down_ref[...], preferred_element_type=jnp.float32).astype(
        jnp.bfloat16
    )


def expert_rows(rows, own, other):
    operands = (rows,) + own + other
    _, width, half = own[0].shape
    wide = pltpu.VMEM((width, 2 * half), jnp.bfloat16)
    return pl.pallas_call(
        expert_kernel,
        in_specs=[HBM] * len(operands),
        out_shape=jax.ShapeDtypeStruct(rows.shape, jnp.bfloat16),
        scratch_shapes=[
            pltpu.VMEM(rows.shape, rows.dtype),
            wide,
            wide,
            pltpu.VMEM((2 * half, width), jnp.bfloat16),
            pltpu.SemaphoreType.DMA((len(operands),)),
        ],
        compiler_params=EXPERT_PARAMS,
        name="expert_rows",
    )(*operands)


def combine_kernel(combine_ref, rows_ref, out_ref):
    out_ref[...] = lax.dot_general(
        combine_ref[...],
        rows_ref[...],
        (((0,), (0,)), ((), ())),
        preferred_element_type=jnp.float32,
    ).astype(jnp.bfloat16)


def combine_rows(combine, rows):
    return pl.pallas_call(
        combine_kernel,
        out_shape=jax.ShapeDtypeStruct((combine.shape[1], rows.shape[1]), jnp.bfloat16),
        compiler_params=PARAMS,
        name="combine_rows",
    )(combine, rows)


def dequant_kernel(place_ref, values_ref, scales_ref, *out_refs):
    rows, width = out_refs[0].shape
    blocks = scales_ref.shape[0]
    column = lax.broadcasted_iota(jnp.int32, (blocks, width), 1) // (width // blocks)
    spread = (column == lax.broadcasted_iota(jnp.int32, (blocks, width), 0)).astype(jnp.bfloat16)
    scales = scales_ref[...]
    high = scales.astype(jnp.bfloat16)
    rest = scales - high.astype(jnp.float32)
    middle = rest.astype(jnp.bfloat16)
    low = (rest - middle.astype(jnp.float32)).astype(jnp.bfloat16)
    wide = sum(
        lax.dot_general(
            part, spread, (((0,), (0,)), ((), ())), preferred_element_type=jnp.float32
        )
        for part in (high, middle, low)
    )
    whole = (values_ref[0].astype(jnp.float32) * wide).astype(jnp.bfloat16)
    for place in range(RADIX):
        block = whole[place * rows : (place + 1) * rows]
        for step, out_ref in enumerate(out_refs):

            @pl.when((place_ref[0] + step) % RADIX == place)
            def _():
                out_ref[...] = block


def dequant(place, values, scales):
    _, rows, width = values.shape
    part = jax.ShapeDtypeStruct((rows // RADIX, width), jnp.bfloat16)
    return pl.pallas_call(
        dequant_kernel,
        in_specs=[SMEM, VMEM, VMEM],
        out_shape=(part,) * RADIX,
        compiler_params=PARAMS,
        name="dequant",
    )(place, values, scales[0].T)


def add_kernel(*refs):
    refs[-1][...] = sum(ref[...].astype(jnp.float32) for ref in refs[:-1]).astype(jnp.bfloat16)


def add_parts(parts):
    return pl.pallas_call(
        add_kernel,
        out_shape=jax.ShapeDtypeStruct(parts[0].shape, jnp.bfloat16),
        compiler_params=PARAMS,
        name="add_parts",
    )(*parts)


def total_kernel(parts_ref, out_ref):
    out_ref[...] = jnp.sum(parts_ref[...].astype(jnp.float32), axis=0).astype(jnp.bfloat16)


def total(parts):
    return pl.pallas_call(
        total_kernel,
        out_shape=jax.ShapeDtypeStruct(parts.shape[1:], jnp.bfloat16),
        compiler_params=PARAMS,
        name="total",
    )(parts)


def update_kernel(replicas, fragment_ref, place_ref, *refs):
    part_refs = refs[:RADIX]
    base_ref, momentum_ref, params_out, momentum_out = refs[RADIX:]
    rows = part_refs[0].shape[0]
    for place in range(RADIX):
        for step, ref in enumerate(part_refs):

            @pl.when((place_ref[0] + RADIX - step) % RADIX == place)
            def _():
                span = pl.ds(place * rows, rows)
                delta = ref[...].astype(jnp.float32) / replicas
                new_momentum = momentum_rate * momentum_ref[span, :] + delta
                momentum_out[span, :] = new_momentum
                params_out[span, :] = base_ref[0, span, :] - outer_rate * (
                    delta + momentum_rate * new_momentum
                )


def update(replicas, place, parts, outer_params, momentum, fragment):
    shape = momentum.shape
    part = parts[0].shape

    def whole(block):
        return pl.BlockSpec(block, lambda i, fragment_ref, place_ref: (0,) * len(block))

    return pl.pallas_call(
        functools.partial(update_kernel, replicas),
        grid_spec=pltpu.PrefetchScalarGridSpec(
            num_scalar_prefetch=2,
            grid=(1,),
            in_specs=[whole(part)] * RADIX
            + [
                pl.BlockSpec(
                    (1,) + shape, lambda i, fragment_ref, place_ref: (fragment_ref[0], 0, 0)
                ),
                whole(shape),
            ],
            out_specs=(whole(shape), whole(shape)),
        ),
        out_shape=(
            jax.ShapeDtypeStruct(shape, jnp.float32),
            jax.ShapeDtypeStruct(shape, jnp.float32),
        ),
        compiler_params=PARAMS,
        name="update",
    )(fragment, place, *parts, outer_params, momentum)


def shift(part, axis, step):
    size = lax.axis_size(axis)
    return lax.ppermute(part, axis, [(i, (i + step) % size) for i in range(size)])


def scatter_stage(parts, axis):
    return [parts[0]] + [shift(parts[step], axis, step) for step in range(1, RADIX)]


def gather_stage(part, axis):
    return [part] + [shift(part, axis, step) for step in range(1, RADIX)]


def place_on(axis):
    return lax.axis_index(axis).astype(jnp.int32).reshape(1)


def exchange(rows, experts):
    width = rows.shape[1]
    return lax.all_to_all(
        rows.reshape(experts, CAP, width), "chip", split_axis=0, concat_axis=0, tiled=True
    ).reshape(experts * CAP, width)


def shards(
    tokens,
    expert_ids,
    route_weights,
    w_gate,
    w_up,
    w_down,
    pseudo_values,
    block_scales,
    outer_params,
    momentum,
    fragment,
):
    experts = lax.axis_size("chip")
    buffer, combine = route(tokens, expert_ids, route_weights, experts)
    mine = exchange(buffer, experts)
    own = (w_gate, w_up, w_down)
    near = place_on("z_near")
    part = add_parts(scatter_stage(dequant(near, pseudo_values, block_scales), "z_near"))
    apart = shift(part, "y_far", 1)
    other = tuple(shift(w, "core", 1) for w in own)
    mine, part = lax.optimization_barrier((mine, part))
    rows = expert_rows(mine, own, other)
    rows, apart = lax.optimization_barrier((rows, apart))
    part = add_parts([part, apart])
    returned = exchange(rows, experts)
    sums = total(lax.all_gather(part, "z_far", axis=0))
    parts = gather_stage(sums, "z_near")
    moe_out = combine_rows(combine, returned)
    parts[0], moe_out = lax.optimization_barrier((parts[0], moe_out))
    new_params, new_momentum = update(
        lax.axis_size(("y_far", "z_far", "z_near")), near, parts, outer_params, momentum, fragment
    )
    return (moe_out, new_params, new_momentum)


def solution(mesh):
    reps, exps = mesh.devices.shape
    fine = Mesh(
        mesh.devices.reshape(reps // (RADIX * RADIX), RADIX, RADIX, exps // 2, 2),
        ("y_far", "z_far", "z_near", "chip", "core"),
    )
    rep = ("y_far", "z_far", "z_near")
    exp = ("chip", "core")
    return jax.shard_map(
        shards,
        mesh=fine,
        in_specs=(
            P(rep + exp, None),
            P(rep + exp, None),
            P(rep + exp, None),
            P(exp, None, None),
            P(exp, None, None),
            P(exp, None, None),
            P(rep, exp, None),
            P(rep, exp, None),
            P(None, exp, None),
            P(exp, None),
            P(),
        ),
        out_specs=(P(rep + exp, None), P(exp, None), P(exp, None)),
        check_vma=False,
    )
```

```python
import functools

import jax
import jax.numpy as jnp
from jax import lax
from jax.experimental import pallas as pl
from jax.experimental.pallas import tpu as pltpu
from jax.sharding import Mesh
from jax.sharding import PartitionSpec as P

CAP = 16
RADIX = 4

momentum_rate = 0.9
outer_rate = 0.7

ROUTE_PARAMS = pltpu.CompilerParams(vmem_limit_bytes=62 * 1024 * 1024)
EXPERT_PARAMS = pltpu.CompilerParams(vmem_limit_bytes=63 * 1024 * 1024)
PARAMS = pltpu.CompilerParams(vmem_limit_bytes=20 * 1024 * 1024)
VMEM = pl.BlockSpec(memory_space=pltpu.VMEM)
HBM = pl.BlockSpec(memory_space=pltpu.HBM)
SMEM = pl.BlockSpec(memory_space=pltpu.SMEM)


def route_kernel(experts, *refs):
    sources, (buffer_ref, combine_ref), targets, sems = refs[:3], refs[3:5], refs[5:8], refs[8]
    fetches = [
        pltpu.make_async_copy(source, target, sems.at[i])
        for i, (source, target) in enumerate(zip(sources, targets))
    ]
    for fetch in fetches:
        fetch.start()
    ids_ref, weights_ref, tokens_ref = targets
    topk, rows = ids_ref.shape
    fetches[0].wait()
    ids = ids_ref[...]
    fetches[1].wait()
    weights = weights_ref[...]
    expert = lax.broadcasted_iota(jnp.int32, (experts, rows), 0)
    named = jnp.zeros((experts, rows), jnp.float32)
    weight = jnp.zeros((experts, rows), jnp.float32)
    for k in range(topk):
        hit = ids[k : k + 1, :] == expert
        named = named + hit.astype(jnp.float32)
        weight = weight + jnp.where(hit, weights[k : k + 1, :], 0.0)
    earlier = lax.broadcasted_iota(jnp.int32, (rows, rows), 0) < lax.broadcasted_iota(
        jnp.int32, (rows, rows), 1
    )
    rank = jnp.dot(
        named.astype(jnp.bfloat16),
        earlier.astype(jnp.bfloat16),
        preferred_element_type=jnp.float32,
    ).astype(jnp.int32)
    rank = jnp.where(named > 0.5, rank, CAP)
    place = lax.broadcasted_iota(jnp.int32, (experts, CAP, rows), 1)
    chosen = rank[:, None, :] == place
    pick = jnp.where(chosen, 1.0, 0.0).reshape(experts * CAP, rows)
    combine_ref[...] = (
        jnp.where(chosen, jnp.broadcast_to(weight[:, None, :], chosen.shape), 0.0)
        .reshape(experts * CAP, rows)
        .astype(jnp.bfloat16)
    )
    fetches[2].wait()
    buffer_ref[...] = jnp.dot(
        pick.astype(jnp.bfloat16), tokens_ref[...], preferred_element_type=jnp.float32
    ).astype(jnp.bfloat16)


def route(tokens, expert_ids, route_weights, experts):
    rows, width = tokens.shape
    operands = (expert_ids.T, route_weights.T, tokens)
    return pl.pallas_call(
        functools.partial(route_kernel, experts),
        out_shape=(
            jax.ShapeDtypeStruct((experts * CAP, width), jnp.bfloat16),
            jax.ShapeDtypeStruct((experts * CAP, rows), jnp.bfloat16),
        ),
        in_specs=[HBM] * len(operands),
        scratch_shapes=[pltpu.VMEM(x.shape, x.dtype) for x in operands]
        + [pltpu.SemaphoreType.DMA((len(operands),))],
        compiler_params=ROUTE_PARAMS,
        name="route",
    )(*operands)


def expert_kernel(rows_hbm, *refs):
    sources, out_ref, targets, sems = refs[:6], refs[6], refs[7:11], refs[11]
    rows_ref, gate_ref, up_ref, down_ref = targets
    half = gate_ref.shape[1] // 2
    moves = [(rows_hbm, rows_ref)]
    for kind, target in enumerate((gate_ref, up_ref, down_ref)):
        for side in range(2):
            span = pl.ds(side * half, half)
            source = sources[3 * side + kind].at[0]
            moves.append((source, target.at[span] if kind == 2 else target.at[:, span]))
    fetches = [
        pltpu.make_async_copy(source, target, sems.at[i])
        for i, (source, target) in enumerate(moves)
    ]
    for fetch in fetches[:5]:
        fetch.start()
    for fetch in fetches[:3]:
        fetch.wait()
    for fetch in fetches[5:]:
        fetch.start()
    rows = rows_ref[...]
    gate = jnp.dot(rows, gate_ref[...], preferred_element_type=jnp.float32)
    for fetch in fetches[3:5]:
        fetch.wait()
    up = jnp.dot(rows, up_ref[...], preferred_element_type=jnp.float32)
    hidden = (gate / (1.0 + jnp.exp(-gate)) * up).astype(jnp.bfloat16)
    for fetch in fetches[5:]:
        fetch.wait()
    out_ref[...] = jnp.dot(hidden, down_ref[...], preferred_element_type=jnp.float32).astype(
        jnp.bfloat16
    )


def expert_rows(rows, own, other):
    operands = (rows,) + own + other
    _, width, half = own[0].shape
    wide = pltpu.VMEM((width, 2 * half), jnp.bfloat16)
    return pl.pallas_call(
        expert_kernel,
        in_specs=[HBM] * len(operands),
        out_shape=jax.ShapeDtypeStruct(rows.shape, jnp.bfloat16),
        scratch_shapes=[
            pltpu.VMEM(rows.shape, rows.dtype),
            wide,
            wide,
            pltpu.VMEM((2 * half, width), jnp.bfloat16),
            pltpu.SemaphoreType.DMA((len(operands),)),
        ],
        compiler_params=EXPERT_PARAMS,
        name="expert_rows",
    )(*operands)


def combine_kernel(combine_ref, rows_ref, out_ref):
    out_ref[...] = lax.dot_general(
        combine_ref[...],
        rows_ref[...],
        (((0,), (0,)), ((), ())),
        preferred_element_type=jnp.float32,
    ).astype(jnp.bfloat16)


def combine_rows(combine, rows):
    return pl.pallas_call(
        combine_kernel,
        out_shape=jax.ShapeDtypeStruct((combine.shape[1], rows.shape[1]), jnp.bfloat16),
        compiler_params=PARAMS,
        name="combine_rows",
    )(combine, rows)


def dequant_kernel(near_ref, values_ref, scales_ref, kept_ref, sent_ref):
    rows = values_ref.shape[1] // RADIX
    blocks, width = scales_ref.shape[0], values_ref.shape[2]
    column = lax.broadcasted_iota(jnp.int32, (blocks, width), 1) // (width // blocks)
    spread = (column == lax.broadcasted_iota(jnp.int32, (blocks, width), 0)).astype(jnp.bfloat16)
    scales = scales_ref[...]
    high = scales.astype(jnp.bfloat16)
    rest = scales - high.astype(jnp.float32)
    middle = rest.astype(jnp.bfloat16)
    low = (rest - middle.astype(jnp.float32)).astype(jnp.bfloat16)
    wide = sum(
        lax.dot_general(
            part, spread, (((0,), (0,)), ((), ())), preferred_element_type=jnp.float32
        )
        for part in (high, middle, low)
    )
    whole = (values_ref[0].astype(jnp.float32) * wide).astype(jnp.bfloat16)
    for bit in range(2):

        @pl.when(near_ref[0] % 2 == bit)
        def _():
            for i in range(RADIX):
                out_ref = kept_ref if i % 2 == bit else sent_ref
                out_ref[i // 2 * rows : (i // 2 + 1) * rows] = whole[i * rows : (i + 1) * rows]


def dequant(near, values, scales):
    _, rows, width = values.shape
    part = jax.ShapeDtypeStruct((rows // 2, width), jnp.bfloat16)
    return pl.pallas_call(
        dequant_kernel,
        in_specs=[SMEM, VMEM, VMEM],
        out_shape=(part, part),
        compiler_params=PARAMS,
        name="dequant",
    )(near, values, scales[0].T)


def add_split_kernel(near_ref, kept_ref, got_ref, own_ref, sent_ref):
    rows = own_ref.shape[0]
    total = (kept_ref[...].astype(jnp.float32) + got_ref[...].astype(jnp.float32)).astype(
        jnp.bfloat16
    )
    for bit in range(2):

        @pl.when(near_ref[0] // 2 == bit)
        def _():
            own_ref[...] = total[bit * rows : (bit + 1) * rows]
            sent_ref[...] = total[(1 - bit) * rows : (2 - bit) * rows]


def add_split(near, kept, got):
    rows, width = kept.shape
    part = jax.ShapeDtypeStruct((rows // 2, width), jnp.bfloat16)
    return pl.pallas_call(
        add_split_kernel,
        in_specs=[SMEM, VMEM, VMEM],
        out_shape=(part, part),
        compiler_params=PARAMS,
        name="add_split",
    )(near, kept, got)


def add_kernel(*refs):
    refs[-1][...] = sum(ref[...].astype(jnp.float32) for ref in refs[:-1]).astype(jnp.bfloat16)


def add_parts(parts):
    return pl.pallas_call(
        add_kernel,
        out_shape=jax.ShapeDtypeStruct(parts[0].shape, jnp.bfloat16),
        compiler_params=PARAMS,
        name="add_parts",
    )(*parts)


def total_kernel(parts_ref, out_ref):
    out_ref[...] = jnp.sum(parts_ref[...].astype(jnp.float32), axis=0).astype(jnp.bfloat16)


def total(parts):
    return pl.pallas_call(
        total_kernel,
        out_shape=jax.ShapeDtypeStruct(parts.shape[1:], jnp.bfloat16),
        compiler_params=PARAMS,
        name="total",
    )(parts)


def update_kernel(replicas, fragment_ref, place_ref, *refs):
    part_refs = refs[:RADIX]
    base_ref, momentum_ref, params_out, momentum_out = refs[RADIX:]
    rows = part_refs[0].shape[0]
    for place in range(RADIX):
        for step, ref in enumerate(part_refs):

            @pl.when((place_ref[0] + RADIX - step) % RADIX == place)
            def _():
                span = pl.ds(place * rows, rows)
                delta = ref[...].astype(jnp.float32) / replicas
                new_momentum = momentum_rate * momentum_ref[span, :] + delta
                momentum_out[span, :] = new_momentum
                params_out[span, :] = base_ref[0, span, :] - outer_rate * (
                    delta + momentum_rate * new_momentum
                )


def update(replicas, place, parts, outer_params, momentum, fragment):
    shape = momentum.shape
    part = parts[0].shape

    def whole(block):
        return pl.BlockSpec(block, lambda i, fragment_ref, place_ref: (0,) * len(block))

    return pl.pallas_call(
        functools.partial(update_kernel, replicas),
        grid_spec=pltpu.PrefetchScalarGridSpec(
            num_scalar_prefetch=2,
            grid=(1,),
            in_specs=[whole(part)] * RADIX
            + [
                pl.BlockSpec(
                    (1,) + shape, lambda i, fragment_ref, place_ref: (fragment_ref[0], 0, 0)
                ),
                whole(shape),
            ],
            out_specs=(whole(shape), whole(shape)),
        ),
        out_shape=(
            jax.ShapeDtypeStruct(shape, jnp.float32),
            jax.ShapeDtypeStruct(shape, jnp.float32),
        ),
        compiler_params=PARAMS,
        name="update",
    )(fragment, place, *parts, outer_params, momentum)


def shift(part, axis, step):
    size = lax.axis_size(axis)
    return lax.ppermute(part, axis, [(i, (i + step) % size) for i in range(size)])


def pair(part, axis, distance):
    return lax.ppermute(part, axis, [(i, i ^ distance) for i in range(lax.axis_size(axis))])


def gather_stage(part, axis):
    return [part] + [shift(part, axis, step) for step in range(1, RADIX)]


def place_on(axis):
    return lax.axis_index(axis).astype(jnp.int32).reshape(1)


def exchange(rows, experts):
    width = rows.shape[1]
    return lax.all_to_all(
        rows.reshape(experts, CAP, width), "chip", split_axis=0, concat_axis=0, tiled=True
    ).reshape(experts * CAP, width)


def shards(
    tokens,
    expert_ids,
    route_weights,
    w_gate,
    w_up,
    w_down,
    pseudo_values,
    block_scales,
    outer_params,
    momentum,
    fragment,
):
    experts = lax.axis_size("chip")
    buffer, combine = route(tokens, expert_ids, route_weights, experts)
    mine = exchange(buffer, experts)
    own = (w_gate, w_up, w_down)
    near = place_on("z_near")
    kept, sent = dequant(near, pseudo_values, block_scales)
    got = pair(sent, "z_near", 1)
    other = tuple(shift(w, "core", 1) for w in own)
    mine_part, sent = add_split(near, kept, got)
    part = add_parts([mine_part, pair(sent, "z_near", 2)])
    apart = shift(part, "y_far", 1)
    mine, part = lax.optimization_barrier((mine, part))
    rows = expert_rows(mine, own, other)
    rows, apart = lax.optimization_barrier((rows, apart))
    part = add_parts([part, apart])
    returned = exchange(rows, experts)
    sums = total(lax.all_gather(part, "z_far", axis=0))
    parts = gather_stage(sums, "z_near")
    moe_out = combine_rows(combine, returned)
    parts[0], moe_out = lax.optimization_barrier((parts[0], moe_out))
    new_params, new_momentum = update(
        lax.axis_size(("y_far", "z_far", "z_near")), near, parts, outer_params, momentum, fragment
    )
    return (moe_out, new_params, new_momentum)


def solution(mesh):
    reps, exps = mesh.devices.shape
    fine = Mesh(
        mesh.devices.reshape(reps // (RADIX * RADIX), RADIX, RADIX, exps // 2, 2),
        ("y_far", "z_far", "z_near", "chip", "core"),
    )
    rep = ("y_far", "z_far", "z_near")
    exp = ("chip", "core")
    return jax.shard_map(
        shards,
        mesh=fine,
        in_specs=(
            P(rep + exp, None),
            P(rep + exp, None),
            P(rep + exp, None),
            P(exp, None, None),
            P(exp, None, None),
            P(exp, None, None),
            P(rep, exp, None),
            P(rep, exp, None),
            P(None, exp, None),
            P(exp, None),
            P(),
        ),
        out_specs=(P(rep + exp, None), P(exp, None), P(exp, None)),
        check_vma=False,
    )
```

```python
import functools

import jax
import jax.numpy as jnp
from jax import lax
from jax.experimental import pallas as pl
from jax.experimental.pallas import tpu as pltpu
from jax.sharding import Mesh
from jax.sharding import PartitionSpec as P

CAP = 16
RADIX = 4

momentum_rate = 0.9
outer_rate = 0.7

ROUTE_PARAMS = pltpu.CompilerParams(vmem_limit_bytes=62 * 1024 * 1024)
EXPERT_PARAMS = pltpu.CompilerParams(vmem_limit_bytes=63 * 1024 * 1024)
PARAMS = pltpu.CompilerParams(vmem_limit_bytes=20 * 1024 * 1024)
VMEM = pl.BlockSpec(memory_space=pltpu.VMEM)
HBM = pl.BlockSpec(memory_space=pltpu.HBM)
SMEM = pl.BlockSpec(memory_space=pltpu.SMEM)


def route_kernel(experts, *refs):
    sources, (buffer_ref, combine_ref), targets, sems = refs[:3], refs[3:5], refs[5:8], refs[8]
    fetches = [
        pltpu.make_async_copy(source, target, sems.at[i])
        for i, (source, target) in enumerate(zip(sources, targets))
    ]
    for fetch in fetches:
        fetch.start()
    ids_ref, weights_ref, tokens_ref = targets
    topk, rows = ids_ref.shape
    fetches[0].wait()
    ids = ids_ref[...]
    fetches[1].wait()
    weights = weights_ref[...]
    expert = lax.broadcasted_iota(jnp.int32, (experts, rows), 0)
    named = jnp.zeros((experts, rows), jnp.float32)
    weight = jnp.zeros((experts, rows), jnp.float32)
    for k in range(topk):
        hit = ids[k : k + 1, :] == expert
        named = named + hit.astype(jnp.float32)
        weight = weight + jnp.where(hit, weights[k : k + 1, :], 0.0)
    earlier = lax.broadcasted_iota(jnp.int32, (rows, rows), 0) < lax.broadcasted_iota(
        jnp.int32, (rows, rows), 1
    )
    rank = jnp.dot(
        named.astype(jnp.bfloat16),
        earlier.astype(jnp.bfloat16),
        preferred_element_type=jnp.float32,
    ).astype(jnp.int32)
    rank = jnp.where(named > 0.5, rank, CAP)
    place = lax.broadcasted_iota(jnp.int32, (experts, CAP, rows), 1)
    chosen = rank[:, None, :] == place
    pick = jnp.where(chosen, 1.0, 0.0).reshape(experts * CAP, rows)
    combine_ref[...] = (
        jnp.where(chosen, jnp.broadcast_to(weight[:, None, :], chosen.shape), 0.0)
        .reshape(experts * CAP, rows)
        .astype(jnp.bfloat16)
    )
    fetches[2].wait()
    buffer_ref[...] = jnp.dot(
        pick.astype(jnp.bfloat16), tokens_ref[...], preferred_element_type=jnp.float32
    ).astype(jnp.bfloat16)


def route(tokens, expert_ids, route_weights, experts):
    rows, width = tokens.shape
    operands = (expert_ids.T, route_weights.T, tokens)
    return pl.pallas_call(
        functools.partial(route_kernel, experts),
        out_shape=(
            jax.ShapeDtypeStruct((experts * CAP, width), jnp.bfloat16),
            jax.ShapeDtypeStruct((experts * CAP, rows), jnp.bfloat16),
        ),
        in_specs=[HBM] * len(operands),
        scratch_shapes=[pltpu.VMEM(x.shape, x.dtype) for x in operands]
        + [pltpu.SemaphoreType.DMA((len(operands),))],
        compiler_params=ROUTE_PARAMS,
        name="route",
    )(*operands)


def expert_kernel(rows_hbm, *refs):
    sources, out_ref, targets, sems = refs[:6], refs[6], refs[7:11], refs[11]
    rows_ref, gate_ref, up_ref, down_ref = targets
    half = gate_ref.shape[1] // 2
    moves = [(rows_hbm, rows_ref)]
    for kind, target in enumerate((gate_ref, up_ref, down_ref)):
        for side in range(2):
            span = pl.ds(side * half, half)
            source = sources[3 * side + kind].at[0]
            moves.append((source, target.at[span] if kind == 2 else target.at[:, span]))
    fetches = [
        pltpu.make_async_copy(source, target, sems.at[i])
        for i, (source, target) in enumerate(moves)
    ]
    for fetch in fetches[:5]:
        fetch.start()
    for fetch in fetches[:3]:
        fetch.wait()
    for fetch in fetches[5:]:
        fetch.start()
    rows = rows_ref[...]
    gate = jnp.dot(rows, gate_ref[...], preferred_element_type=jnp.float32)
    for fetch in fetches[3:5]:
        fetch.wait()
    up = jnp.dot(rows, up_ref[...], preferred_element_type=jnp.float32)
    hidden = (gate / (1.0 + jnp.exp(-gate)) * up).astype(jnp.bfloat16)
    for fetch in fetches[5:]:
        fetch.wait()
    out_ref[...] = jnp.dot(hidden, down_ref[...], preferred_element_type=jnp.float32).astype(
        jnp.bfloat16
    )


def expert_rows(rows, own, other):
    operands = (rows,) + own + other
    _, width, half = own[0].shape
    wide = pltpu.VMEM((width, 2 * half), jnp.bfloat16)
    return pl.pallas_call(
        expert_kernel,
        in_specs=[HBM] * len(operands),
        out_shape=jax.ShapeDtypeStruct(rows.shape, jnp.bfloat16),
        scratch_shapes=[
            pltpu.VMEM(rows.shape, rows.dtype),
            wide,
            wide,
            pltpu.VMEM((2 * half, width), jnp.bfloat16),
            pltpu.SemaphoreType.DMA((len(operands),)),
        ],
        compiler_params=EXPERT_PARAMS,
        name="expert_rows",
    )(*operands)


def combine_kernel(combine_ref, rows_ref, out_ref):
    out_ref[...] = lax.dot_general(
        combine_ref[...],
        rows_ref[...],
        (((0,), (0,)), ((), ())),
        preferred_element_type=jnp.float32,
    ).astype(jnp.bfloat16)


def combine_rows(combine, rows):
    return pl.pallas_call(
        combine_kernel,
        out_shape=jax.ShapeDtypeStruct((combine.shape[1], rows.shape[1]), jnp.bfloat16),
        compiler_params=PARAMS,
        name="combine_rows",
    )(combine, rows)


def dequant_kernel(place_ref, values_ref, scales_ref, *out_refs):
    rows, width = out_refs[0].shape
    blocks = scales_ref.shape[0]
    column = lax.broadcasted_iota(jnp.int32, (blocks, width), 1) // (width // blocks)
    spread = (column == lax.broadcasted_iota(jnp.int32, (blocks, width), 0)).astype(jnp.bfloat16)
    scales = scales_ref[...]
    high = scales.astype(jnp.bfloat16)
    rest = scales - high.astype(jnp.float32)
    middle = rest.astype(jnp.bfloat16)
    low = (rest - middle.astype(jnp.float32)).astype(jnp.bfloat16)
    wide = sum(
        lax.dot_general(
            part, spread, (((0,), (0,)), ((), ())), preferred_element_type=jnp.float32
        )
        for part in (high, middle, low)
    )
    whole = (values_ref[0].astype(jnp.float32) * wide).astype(jnp.bfloat16)
    for place in range(RADIX):
        block = whole[place * rows : (place + 1) * rows]
        for step, out_ref in enumerate(out_refs):

            @pl.when((place_ref[0] + step) % RADIX == place)
            def _():
                out_ref[...] = block


def dequant(place, values, scales):
    _, rows, width = values.shape
    part = jax.ShapeDtypeStruct((rows // RADIX, width), jnp.bfloat16)
    return pl.pallas_call(
        dequant_kernel,
        in_specs=[SMEM, VMEM, VMEM],
        out_shape=(part,) * RADIX,
        compiler_params=PARAMS,
        name="dequant",
    )(place, values, scales[0].T)


def add_kernel(*refs):
    refs[-1][...] = sum(ref[...].astype(jnp.float32) for ref in refs[:-1]).astype(jnp.bfloat16)


def add_parts(parts):
    return pl.pallas_call(
        add_kernel,
        out_shape=jax.ShapeDtypeStruct(parts[0].shape, jnp.bfloat16),
        compiler_params=PARAMS,
        name="add_parts",
    )(*parts)


def total_kernel(parts_ref, out_ref):
    out_ref[...] = jnp.sum(parts_ref[...].astype(jnp.float32), axis=0).astype(jnp.bfloat16)


def total(parts):
    return pl.pallas_call(
        total_kernel,
        out_shape=jax.ShapeDtypeStruct(parts.shape[1:], jnp.bfloat16),
        compiler_params=PARAMS,
        name="total",
    )(parts)


def update_kernel(replicas, fragment_ref, place_ref, *refs):
    part_refs = refs[:RADIX]
    base_ref, momentum_ref, params_out, momentum_out = refs[RADIX:]
    rows = part_refs[0].shape[0]
    for place in range(RADIX):
        for step, ref in enumerate(part_refs):

            @pl.when((place_ref[0] + RADIX - step) % RADIX == place)
            def _():
                span = pl.ds(place * rows, rows)
                delta = ref[...].astype(jnp.float32) / replicas
                new_momentum = momentum_rate * momentum_ref[span, :] + delta
                momentum_out[span, :] = new_momentum
                params_out[span, :] = base_ref[0, span, :] - outer_rate * (
                    delta + momentum_rate * new_momentum
                )


def update(replicas, place, parts, outer_params, momentum, fragment):
    shape = momentum.shape
    part = parts[0].shape

    def whole(block):
        return pl.BlockSpec(block, lambda i, fragment_ref, place_ref: (0,) * len(block))

    return pl.pallas_call(
        functools.partial(update_kernel, replicas),
        grid_spec=pltpu.PrefetchScalarGridSpec(
            num_scalar_prefetch=2,
            grid=(1,),
            in_specs=[whole(part)] * RADIX
            + [
                pl.BlockSpec(
                    (1,) + shape, lambda i, fragment_ref, place_ref: (fragment_ref[0], 0, 0)
                ),
                whole(shape),
            ],
            out_specs=(whole(shape), whole(shape)),
        ),
        out_shape=(
            jax.ShapeDtypeStruct(shape, jnp.float32),
            jax.ShapeDtypeStruct(shape, jnp.float32),
        ),
        compiler_params=PARAMS,
        name="update",
    )(fragment, place, *parts, outer_params, momentum)


def shift(part, axis, step):
    size = lax.axis_size(axis)
    return lax.ppermute(part, axis, [(i, (i + step) % size) for i in range(size)])


def scatter_stage(parts, axis):
    return [parts[0]] + [shift(parts[step], axis, step) for step in range(1, RADIX)]


def gather_stage(part, axis):
    return [part] + [shift(part, axis, step) for step in range(1, RADIX)]


def place_on(axis):
    return lax.axis_index(axis).astype(jnp.int32).reshape(1)


def exchange(rows, experts):
    width = rows.shape[1]
    return lax.all_to_all(
        rows.reshape(experts, CAP, width), "chip", split_axis=0, concat_axis=0, tiled=True
    ).reshape(experts * CAP, width)


def shards(
    tokens,
    expert_ids,
    route_weights,
    w_gate,
    w_up,
    w_down,
    pseudo_values,
    block_scales,
    outer_params,
    momentum,
    fragment,
):
    experts = lax.axis_size("chip")
    buffer, combine = route(tokens, expert_ids, route_weights, experts)
    mine = exchange(buffer, experts)
    own = (w_gate, w_up, w_down)
    near = place_on("z_near")
    part = add_parts(scatter_stage(dequant(near, pseudo_values, block_scales), "z_near"))
    part, down = lax.optimization_barrier((part, w_down))
    other = (shift(w_gate, "core", 1), shift(w_up, "core", 1), shift(down, "core", 1))
    apart = shift(part, "y_far", 1)
    mine, part = lax.optimization_barrier((mine, part))
    rows = expert_rows(mine, own, other)
    rows, apart = lax.optimization_barrier((rows, apart))
    part = add_parts([part, apart])
    returned = exchange(rows, experts)
    sums = total(lax.all_gather(part, "z_far", axis=0))
    parts = gather_stage(sums, "z_near")
    moe_out = combine_rows(combine, returned)
    parts[0], moe_out = lax.optimization_barrier((parts[0], moe_out))
    new_params, new_momentum = update(
        lax.axis_size(("y_far", "z_far", "z_near")), near, parts, outer_params, momentum, fragment
    )
    return (moe_out, new_params, new_momentum)


def solution(mesh):
    reps, exps = mesh.devices.shape
    fine = Mesh(
        mesh.devices.reshape(reps // (RADIX * RADIX), RADIX, RADIX, exps // 2, 2),
        ("y_far", "z_far", "z_near", "chip", "core"),
    )
    rep = ("y_far", "z_far", "z_near")
    exp = ("chip", "core")
    return jax.shard_map(
        shards,
        mesh=fine,
        in_specs=(
            P(rep + exp, None),
            P(rep + exp, None),
            P(rep + exp, None),
            P(exp, None, None),
            P(exp, None, None),
            P(exp, None, None),
            P(rep, exp, None),
            P(rep, exp, None),
            P(None, exp, None),
            P(exp, None),
            P(),
        ),
        out_specs=(P(rep + exp, None), P(exp, None), P(exp, None)),
        check_vma=False,
    )
```

```python
import functools

import jax
import jax.numpy as jnp
from jax import lax
from jax.experimental import pallas as pl
from jax.experimental.pallas import tpu as pltpu
from jax.sharding import Mesh
from jax.sharding import PartitionSpec as P

CAP = 16
RADIX = 4
CHUNKS = 4

momentum_rate = 0.9
outer_rate = 0.7

ROUTE_PARAMS = pltpu.CompilerParams(vmem_limit_bytes=62 * 1024 * 1024)
EXPERT_PARAMS = pltpu.CompilerParams(vmem_limit_bytes=63 * 1024 * 1024)
PARAMS = pltpu.CompilerParams(vmem_limit_bytes=20 * 1024 * 1024)
VMEM = pl.BlockSpec(memory_space=pltpu.VMEM)
HBM = pl.BlockSpec(memory_space=pltpu.HBM)
SMEM = pl.BlockSpec(memory_space=pltpu.SMEM)


def route_kernel(experts, *refs):
    sources, (buffer_ref, combine_ref), targets, sems = refs[:3], refs[3:5], refs[5:8], refs[8]
    fetches = [
        pltpu.make_async_copy(source, target, sems.at[i])
        for i, (source, target) in enumerate(zip(sources, targets))
    ]
    for fetch in fetches:
        fetch.start()
    ids_ref, weights_ref, tokens_ref = targets
    topk, rows = ids_ref.shape
    fetches[0].wait()
    ids = ids_ref[...]
    fetches[1].wait()
    weights = weights_ref[...]
    expert = lax.broadcasted_iota(jnp.int32, (experts, rows), 0)
    named = jnp.zeros((experts, rows), jnp.float32)
    weight = jnp.zeros((experts, rows), jnp.float32)
    for k in range(topk):
        hit = ids[k : k + 1, :] == expert
        named = named + hit.astype(jnp.float32)
        weight = weight + jnp.where(hit, weights[k : k + 1, :], 0.0)
    earlier = lax.broadcasted_iota(jnp.int32, (rows, rows), 0) < lax.broadcasted_iota(
        jnp.int32, (rows, rows), 1
    )
    rank = jnp.dot(
        named.astype(jnp.bfloat16),
        earlier.astype(jnp.bfloat16),
        preferred_element_type=jnp.float32,
    ).astype(jnp.int32)
    rank = jnp.where(named > 0.5, rank, CAP)
    place = lax.broadcasted_iota(jnp.int32, (experts, CAP, rows), 1)
    chosen = rank[:, None, :] == place
    pick = jnp.where(chosen, 1.0, 0.0).reshape(experts * CAP, rows)
    combine_ref[...] = (
        jnp.where(chosen, jnp.broadcast_to(weight[:, None, :], chosen.shape), 0.0)
        .reshape(experts * CAP, rows)
        .astype(jnp.bfloat16)
    )
    fetches[2].wait()
    buffer_ref[...] = jnp.dot(
        pick.astype(jnp.bfloat16), tokens_ref[...], preferred_element_type=jnp.float32
    ).astype(jnp.bfloat16)


def route(tokens, expert_ids, route_weights, experts):
    rows, width = tokens.shape
    operands = (expert_ids.T, route_weights.T, tokens)
    return pl.pallas_call(
        functools.partial(route_kernel, experts),
        out_shape=(
            jax.ShapeDtypeStruct((experts * CAP, width), jnp.bfloat16),
            jax.ShapeDtypeStruct((experts * CAP, rows), jnp.bfloat16),
        ),
        in_specs=[HBM] * len(operands),
        scratch_shapes=[pltpu.VMEM(x.shape, x.dtype) for x in operands]
        + [pltpu.SemaphoreType.DMA((len(operands),))],
        compiler_params=ROUTE_PARAMS,
        name="route",
    )(*operands)


def expert_kernel(rows_hbm, *refs):
    sources, out_ref, targets, sems = refs[:6], refs[6], refs[7:11], refs[11]
    rows_ref, gate_ref, up_ref, down_ref = targets
    half = gate_ref.shape[1] // 2
    depth = rows_ref.shape[1] // CHUNKS
    sides = [pl.ds(side * half, half) for side in range(2)]
    stages = []
    for chunk in range(CHUNKS):
        deep = pl.ds(chunk * depth, depth)
        stage = [(rows_hbm.at[:, deep], rows_ref.at[:, deep])]
        for kind, target in enumerate((gate_ref, up_ref)):
            for side, span in enumerate(sides):
                stage.append((sources[3 * side + kind].at[0, deep], target.at[deep, span]))
        stages.append(stage)
    stages.append([(sources[3 * side + 2].at[0], down_ref.at[sides[side]]) for side in range(2)])
    fetches = []
    for stage in stages:
        first = sum(len(done) for done in fetches)
        fetches.append(
            [
                pltpu.make_async_copy(source, target, sems.at[first + i])
                for i, (source, target) in enumerate(stage)
            ]
        )
    for stage in fetches[:2]:
        for fetch in stage:
            fetch.start()
    gate = up = None
    for chunk in range(CHUNKS):
        for fetch in fetches[chunk]:
            fetch.wait()
        if chunk + 2 < len(fetches):
            for fetch in fetches[chunk + 2]:
                fetch.start()
        deep = slice(chunk * depth, (chunk + 1) * depth)
        rows = rows_ref[:, deep]
        gate_part = jnp.dot(rows, gate_ref[deep], preferred_element_type=jnp.float32)
        up_part = jnp.dot(rows, up_ref[deep], preferred_element_type=jnp.float32)
        gate = gate_part if gate is None else gate + gate_part
        up = up_part if up is None else up + up_part
    hidden = (gate / (1.0 + jnp.exp(-gate)) * up).astype(jnp.bfloat16)
    for fetch in fetches[CHUNKS]:
        fetch.wait()
    out_ref[...] = jnp.dot(hidden, down_ref[...], preferred_element_type=jnp.float32).astype(
        jnp.bfloat16
    )


def expert_rows(rows, own, other):
    operands = (rows,) + own + other
    _, width, half = own[0].shape
    wide = pltpu.VMEM((width, 2 * half), jnp.bfloat16)
    return pl.pallas_call(
        expert_kernel,
        in_specs=[HBM] * len(operands),
        out_shape=jax.ShapeDtypeStruct(rows.shape, jnp.bfloat16),
        scratch_shapes=[
            pltpu.VMEM(rows.shape, rows.dtype),
            wide,
            wide,
            pltpu.VMEM((2 * half, width), jnp.bfloat16),
            pltpu.SemaphoreType.DMA((5 * CHUNKS + 2,)),
        ],
        compiler_params=EXPERT_PARAMS,
        name="expert_rows",
    )(*operands)


def combine_kernel(combine_ref, rows_ref, out_ref):
    out_ref[...] = lax.dot_general(
        combine_ref[...],
        rows_ref[...],
        (((0,), (0,)), ((), ())),
        preferred_element_type=jnp.float32,
    ).astype(jnp.bfloat16)


def combine_rows(combine, rows):
    return pl.pallas_call(
        combine_kernel,
        out_shape=jax.ShapeDtypeStruct((combine.shape[1], rows.shape[1]), jnp.bfloat16),
        compiler_params=PARAMS,
        name="combine_rows",
    )(combine, rows)


def dequant_kernel(place_ref, values_ref, scales_ref, *out_refs):
    rows, width = out_refs[0].shape
    blocks = scales_ref.shape[0]
    column = lax.broadcasted_iota(jnp.int32, (blocks, width), 1) // (width // blocks)
    spread = (column == lax.broadcasted_iota(jnp.int32, (blocks, width), 0)).astype(jnp.bfloat16)
    scales = scales_ref[...]
    high = scales.astype(jnp.bfloat16)
    rest = scales - high.astype(jnp.float32)
    middle = rest.astype(jnp.bfloat16)
    low = (rest - middle.astype(jnp.float32)).astype(jnp.bfloat16)
    wide = sum(
        lax.dot_general(
            part, spread, (((0,), (0,)), ((), ())), preferred_element_type=jnp.float32
        )
        for part in (high, middle, low)
    )
    whole = (values_ref[0].astype(jnp.float32) * wide).astype(jnp.bfloat16)
    for place in range(RADIX):
        block = whole[place * rows : (place + 1) * rows]
        for step, out_ref in enumerate(out_refs):

            @pl.when((place_ref[0] + step) % RADIX == place)
            def _():
                out_ref[...] = block


def dequant(place, values, scales):
    _, rows, width = values.shape
    part = jax.ShapeDtypeStruct((rows // RADIX, width), jnp.bfloat16)
    return pl.pallas_call(
        dequant_kernel,
        in_specs=[SMEM, VMEM, VMEM],
        out_shape=(part,) * RADIX,
        compiler_params=PARAMS,
        name="dequant",
    )(place, values, scales[0].T)


def add_kernel(*refs):
    refs[-1][...] = sum(ref[...].astype(jnp.float32) for ref in refs[:-1]).astype(jnp.bfloat16)


def add_parts(parts):
    return pl.pallas_call(
        add_kernel,
        out_shape=jax.ShapeDtypeStruct(parts[0].shape, jnp.bfloat16),
        compiler_params=PARAMS,
        name="add_parts",
    )(*parts)


def total_kernel(parts_ref, out_ref):
    out_ref[...] = jnp.sum(parts_ref[...].astype(jnp.float32), axis=0).astype(jnp.bfloat16)


def total(parts):
    return pl.pallas_call(
        total_kernel,
        out_shape=jax.ShapeDtypeStruct(parts.shape[1:], jnp.bfloat16),
        compiler_params=PARAMS,
        name="total",
    )(parts)


def update_kernel(replicas, fragment_ref, place_ref, *refs):
    part_refs = refs[:RADIX]
    base_ref, momentum_ref, params_out, momentum_out = refs[RADIX:]
    rows = part_refs[0].shape[0]
    for place in range(RADIX):
        for step, ref in enumerate(part_refs):

            @pl.when((place_ref[0] + RADIX - step) % RADIX == place)
            def _():
                span = pl.ds(place * rows, rows)
                delta = ref[...].astype(jnp.float32) / replicas
                new_momentum = momentum_rate * momentum_ref[span, :] + delta
                momentum_out[span, :] = new_momentum
                params_out[span, :] = base_ref[0, span, :] - outer_rate * (
                    delta + momentum_rate * new_momentum
                )


def update(replicas, place, parts, outer_params, momentum, fragment):
    shape = momentum.shape
    part = parts[0].shape

    def whole(block):
        return pl.BlockSpec(block, lambda i, fragment_ref, place_ref: (0,) * len(block))

    return pl.pallas_call(
        functools.partial(update_kernel, replicas),
        grid_spec=pltpu.PrefetchScalarGridSpec(
            num_scalar_prefetch=2,
            grid=(1,),
            in_specs=[whole(part)] * RADIX
            + [
                pl.BlockSpec(
                    (1,) + shape, lambda i, fragment_ref, place_ref: (fragment_ref[0], 0, 0)
                ),
                whole(shape),
            ],
            out_specs=(whole(shape), whole(shape)),
        ),
        out_shape=(
            jax.ShapeDtypeStruct(shape, jnp.float32),
            jax.ShapeDtypeStruct(shape, jnp.float32),
        ),
        compiler_params=PARAMS,
        name="update",
    )(fragment, place, *parts, outer_params, momentum)


def shift(part, axis, step):
    size = lax.axis_size(axis)
    return lax.ppermute(part, axis, [(i, (i + step) % size) for i in range(size)])


def scatter_stage(parts, axis):
    return [parts[0]] + [shift(parts[step], axis, step) for step in range(1, RADIX)]


def gather_stage(part, axis):
    return [part] + [shift(part, axis, step) for step in range(1, RADIX)]


def place_on(axis):
    return lax.axis_index(axis).astype(jnp.int32).reshape(1)


def exchange(rows, experts):
    width = rows.shape[1]
    return lax.all_to_all(
        rows.reshape(experts, CAP, width), "chip", split_axis=0, concat_axis=0, tiled=True
    ).reshape(experts * CAP, width)


def shards(
    tokens,
    expert_ids,
    route_weights,
    w_gate,
    w_up,
    w_down,
    pseudo_values,
    block_scales,
    outer_params,
    momentum,
    fragment,
):
    experts = lax.axis_size("chip")
    buffer, combine = route(tokens, expert_ids, route_weights, experts)
    mine = exchange(buffer, experts)
    own = (w_gate, w_up, w_down)
    near = place_on("z_near")
    part = add_parts(scatter_stage(dequant(near, pseudo_values, block_scales), "z_near"))
    part, down = lax.optimization_barrier((part, w_down))
    other = (shift(w_gate, "core", 1), shift(w_up, "core", 1), shift(down, "core", 1))
    apart = shift(part, "y_far", 1)
    mine, part = lax.optimization_barrier((mine, part))
    rows = expert_rows(mine, own, other)
    rows, apart = lax.optimization_barrier((rows, apart))
    part = add_parts([part, apart])
    returned = exchange(rows, experts)
    sums = total(lax.all_gather(part, "z_far", axis=0))
    parts = gather_stage(sums, "z_near")
    moe_out = combine_rows(combine, returned)
    parts[0], moe_out = lax.optimization_barrier((parts[0], moe_out))
    new_params, new_momentum = update(
        lax.axis_size(("y_far", "z_far", "z_near")), near, parts, outer_params, momentum, fragment
    )
    return (moe_out, new_params, new_momentum)


def solution(mesh):
    reps, exps = mesh.devices.shape
    fine = Mesh(
        mesh.devices.reshape(reps // (RADIX * RADIX), RADIX, RADIX, exps // 2, 2),
        ("y_far", "z_far", "z_near", "chip", "core"),
    )
    rep = ("y_far", "z_far", "z_near")
    exp = ("chip", "core")
    return jax.shard_map(
        shards,
        mesh=fine,
        in_specs=(
            P(rep + exp, None),
            P(rep + exp, None),
            P(rep + exp, None),
            P(exp, None, None),
            P(exp, None, None),
            P(exp, None, None),
            P(rep, exp, None),
            P(rep, exp, None),
            P(None, exp, None),
            P(exp, None),
            P(),
        ),
        out_specs=(P(rep + exp, None), P(exp, None), P(exp, None)),
        check_vma=False,
    )
```

```python
import functools

import jax
import jax.numpy as jnp
from jax import lax
from jax.experimental import pallas as pl
from jax.experimental.pallas import tpu as pltpu
from jax.sharding import Mesh
from jax.sharding import PartitionSpec as P

CAP = 16
RADIX = 4

momentum_rate = 0.9
outer_rate = 0.7

ROUTE_PARAMS = pltpu.CompilerParams(vmem_limit_bytes=62 * 1024 * 1024)
EXPERT_PARAMS = pltpu.CompilerParams(vmem_limit_bytes=63 * 1024 * 1024)
PARAMS = pltpu.CompilerParams(vmem_limit_bytes=20 * 1024 * 1024)
VMEM = pl.BlockSpec(memory_space=pltpu.VMEM)
HBM = pl.BlockSpec(memory_space=pltpu.HBM)
SMEM = pl.BlockSpec(memory_space=pltpu.SMEM)


def route_kernel(experts, *refs):
    sources, (buffer_ref, combine_ref), targets, sems = refs[:3], refs[3:5], refs[5:8], refs[8]
    fetches = [
        pltpu.make_async_copy(source, target, sems.at[i])
        for i, (source, target) in enumerate(zip(sources, targets))
    ]
    for fetch in fetches:
        fetch.start()
    ids_ref, weights_ref, tokens_ref = targets
    topk, rows = ids_ref.shape
    fetches[0].wait()
    ids = ids_ref[...]
    fetches[1].wait()
    weights = weights_ref[...]
    expert = lax.broadcasted_iota(jnp.int32, (experts, rows), 0)
    named = jnp.zeros((experts, rows), jnp.float32)
    weight = jnp.zeros((experts, rows), jnp.float32)
    for k in range(topk):
        hit = ids[k : k + 1, :] == expert
        named = named + hit.astype(jnp.float32)
        weight = weight + jnp.where(hit, weights[k : k + 1, :], 0.0)
    earlier = lax.broadcasted_iota(jnp.int32, (rows, rows), 0) < lax.broadcasted_iota(
        jnp.int32, (rows, rows), 1
    )
    rank = jnp.dot(
        named.astype(jnp.bfloat16),
        earlier.astype(jnp.bfloat16),
        preferred_element_type=jnp.float32,
    ).astype(jnp.int32)
    rank = jnp.where(named > 0.5, rank, CAP)
    place = lax.broadcasted_iota(jnp.int32, (experts, CAP, rows), 1)
    chosen = rank[:, None, :] == place
    pick = jnp.where(chosen, 1.0, 0.0).reshape(experts * CAP, rows)
    combine_ref[...] = (
        jnp.where(chosen, jnp.broadcast_to(weight[:, None, :], chosen.shape), 0.0)
        .reshape(experts * CAP, rows)
        .astype(jnp.bfloat16)
    )
    fetches[2].wait()
    buffer_ref[...] = jnp.dot(
        pick.astype(jnp.bfloat16), tokens_ref[...], preferred_element_type=jnp.float32
    ).astype(jnp.bfloat16)


def route(tokens, expert_ids, route_weights, experts):
    rows, width = tokens.shape
    operands = (expert_ids.T, route_weights.T, tokens)
    return pl.pallas_call(
        functools.partial(route_kernel, experts),
        out_shape=(
            jax.ShapeDtypeStruct((experts * CAP, width), jnp.bfloat16),
            jax.ShapeDtypeStruct((experts * CAP, rows), jnp.bfloat16),
        ),
        in_specs=[HBM] * len(operands),
        scratch_shapes=[pltpu.VMEM(x.shape, x.dtype) for x in operands]
        + [pltpu.SemaphoreType.DMA((len(operands),))],
        compiler_params=ROUTE_PARAMS,
        name="route",
    )(*operands)


def expert_kernel(rows_hbm, *refs):
    sources, out_ref, targets, sems = refs[:6], refs[6], refs[7:11], refs[11]
    rows_ref, gate_ref, up_ref, down_ref = targets
    half = gate_ref.shape[1] // 2
    moves = [(rows_hbm, rows_ref)]
    for kind, target in enumerate((gate_ref, up_ref, down_ref)):
        for side in range(2):
            span = pl.ds(side * half, half)
            source = sources[3 * side + kind].at[0]
            moves.append((source, target.at[span] if kind == 2 else target.at[:, span]))
    fetches = [
        pltpu.make_async_copy(source, target, sems.at[i])
        for i, (source, target) in enumerate(moves)
    ]
    for fetch in fetches[:5]:
        fetch.start()
    for fetch in fetches[:3]:
        fetch.wait()
    for fetch in fetches[5:]:
        fetch.start()
    rows = rows_ref[...]
    gate = jnp.dot(rows, gate_ref[...], preferred_element_type=jnp.float32)
    for fetch in fetches[3:5]:
        fetch.wait()
    up = jnp.dot(rows, up_ref[...], preferred_element_type=jnp.float32)
    hidden = (gate / (1.0 + jnp.exp(-gate)) * up).astype(jnp.bfloat16)
    for fetch in fetches[5:]:
        fetch.wait()
    out_ref[...] = jnp.dot(hidden, down_ref[...], preferred_element_type=jnp.float32).astype(
        jnp.bfloat16
    )


def expert_rows(rows, own, other):
    operands = (rows,) + own + other
    _, width, half = own[0].shape
    wide = pltpu.VMEM((width, 2 * half), jnp.bfloat16)
    return pl.pallas_call(
        expert_kernel,
        in_specs=[HBM] * len(operands),
        out_shape=jax.ShapeDtypeStruct(rows.shape, jnp.bfloat16),
        scratch_shapes=[
            pltpu.VMEM(rows.shape, rows.dtype),
            wide,
            wide,
            pltpu.VMEM((2 * half, width), jnp.bfloat16),
            pltpu.SemaphoreType.DMA((len(operands),)),
        ],
        compiler_params=EXPERT_PARAMS,
        name="expert_rows",
    )(*operands)


def combine_kernel(combine_ref, rows_ref, out_ref):
    out_ref[...] = lax.dot_general(
        combine_ref[...],
        rows_ref[...],
        (((0,), (0,)), ((), ())),
        preferred_element_type=jnp.float32,
    ).astype(jnp.bfloat16)


def combine_rows(combine, rows):
    return pl.pallas_call(
        combine_kernel,
        out_shape=jax.ShapeDtypeStruct((combine.shape[1], rows.shape[1]), jnp.bfloat16),
        compiler_params=PARAMS,
        name="combine_rows",
    )(combine, rows)


def dequant_kernel(place_ref, values_ref, scales_ref, *out_refs):
    rows, width = out_refs[0].shape
    blocks = scales_ref.shape[0]
    column = lax.broadcasted_iota(jnp.int32, (blocks, width), 1) // (width // blocks)
    spread = (column == lax.broadcasted_iota(jnp.int32, (blocks, width), 0)).astype(jnp.bfloat16)
    scales = scales_ref[...]
    high = scales.astype(jnp.bfloat16)
    rest = scales - high.astype(jnp.float32)
    middle = rest.astype(jnp.bfloat16)
    low = (rest - middle.astype(jnp.float32)).astype(jnp.bfloat16)
    wide = sum(
        lax.dot_general(
            part, spread, (((0,), (0,)), ((), ())), preferred_element_type=jnp.float32
        )
        for part in (high, middle, low)
    )
    whole = (values_ref[0].astype(jnp.float32) * wide).astype(jnp.bfloat16)
    for place in range(RADIX):
        block = whole[place * rows : (place + 1) * rows]
        for step, out_ref in enumerate(out_refs):

            @pl.when((place_ref[0] + step) % RADIX == place)
            def _():
                out_ref[...] = block


def dequant(place, values, scales):
    _, rows, width = values.shape
    part = jax.ShapeDtypeStruct((rows // RADIX, width), jnp.bfloat16)
    return pl.pallas_call(
        dequant_kernel,
        in_specs=[SMEM, VMEM, VMEM],
        out_shape=(part,) * RADIX,
        compiler_params=PARAMS,
        name="dequant",
    )(place, values, scales[0].T)


def add_kernel(*refs):
    refs[-1][...] = sum(ref[...].astype(jnp.float32) for ref in refs[:-1]).astype(jnp.bfloat16)


def add_parts(parts):
    return pl.pallas_call(
        add_kernel,
        out_shape=jax.ShapeDtypeStruct(parts[0].shape, jnp.bfloat16),
        compiler_params=PARAMS,
        name="add_parts",
    )(*parts)


def total_kernel(parts_ref, out_ref):
    out_ref[...] = jnp.sum(parts_ref[...].astype(jnp.float32), axis=0).astype(jnp.bfloat16)


def total(parts):
    return pl.pallas_call(
        total_kernel,
        out_shape=jax.ShapeDtypeStruct(parts.shape[1:], jnp.bfloat16),
        compiler_params=PARAMS,
        name="total",
    )(parts)


def update_kernel(replicas, fragment_ref, place_ref, *refs):
    part_refs = refs[:RADIX]
    base_ref, momentum_ref, params_out, momentum_out = refs[RADIX:]
    rows = part_refs[0].shape[0]
    for place in range(RADIX):
        for step, ref in enumerate(part_refs):

            @pl.when((place_ref[0] + RADIX - step) % RADIX == place)
            def _():
                span = pl.ds(place * rows, rows)
                delta = ref[...].astype(jnp.float32) / replicas
                new_momentum = momentum_rate * momentum_ref[span, :] + delta
                momentum_out[span, :] = new_momentum
                params_out[span, :] = base_ref[0, span, :] - outer_rate * (
                    delta + momentum_rate * new_momentum
                )


def update(replicas, place, parts, outer_params, momentum, fragment):
    shape = momentum.shape
    part = parts[0].shape

    def whole(block):
        return pl.BlockSpec(block, lambda i, fragment_ref, place_ref: (0,) * len(block))

    return pl.pallas_call(
        functools.partial(update_kernel, replicas),
        grid_spec=pltpu.PrefetchScalarGridSpec(
            num_scalar_prefetch=2,
            grid=(1,),
            in_specs=[whole(part)] * RADIX
            + [
                pl.BlockSpec(
                    (1,) + shape, lambda i, fragment_ref, place_ref: (fragment_ref[0], 0, 0)
                ),
                whole(shape),
            ],
            out_specs=(whole(shape), whole(shape)),
        ),
        out_shape=(
            jax.ShapeDtypeStruct(shape, jnp.float32),
            jax.ShapeDtypeStruct(shape, jnp.float32),
        ),
        compiler_params=PARAMS,
        name="update",
    )(fragment, place, *parts, outer_params, momentum)


def shift(part, axis, step):
    size = lax.axis_size(axis)
    return lax.ppermute(part, axis, [(i, (i + step) % size) for i in range(size)])


def scatter_stage(parts, axis):
    return [parts[0]] + [shift(parts[step], axis, step) for step in range(1, RADIX)]


def gather_stage(part, axis):
    return [part] + [shift(part, axis, step) for step in range(1, RADIX)]


def place_on(axis):
    return lax.axis_index(axis).astype(jnp.int32).reshape(1)


def exchange(rows, experts):
    width = rows.shape[1]
    return lax.all_to_all(
        rows.reshape(experts, CAP, width), "chip", split_axis=0, concat_axis=0, tiled=True
    ).reshape(experts * CAP, width)


def shards(
    tokens,
    expert_ids,
    route_weights,
    w_gate,
    w_up,
    w_down,
    pseudo_values,
    block_scales,
    outer_params,
    momentum,
    fragment,
):
    experts = lax.axis_size("chip")
    buffer, combine = route(tokens, expert_ids, route_weights, experts)
    mine = exchange(buffer, experts)
    own = (w_gate, w_up, w_down)
    near = place_on("z_near")
    part = add_parts(scatter_stage(dequant(near, pseudo_values, block_scales), "z_near"))
    part, sent = lax.optimization_barrier((part, own))
    other = tuple(shift(w, "core", 1) for w in sent)
    apart = shift(part, "y_far", 1)
    mine, part = lax.optimization_barrier((mine, part))
    rows = expert_rows(mine, own, other)
    rows, apart = lax.optimization_barrier((rows, apart))
    part = add_parts([part, apart])
    returned = exchange(rows, experts)
    sums = total(lax.all_gather(part, "z_far", axis=0))
    parts = gather_stage(sums, "z_near")
    moe_out = combine_rows(combine, returned)
    parts[0], moe_out = lax.optimization_barrier((parts[0], moe_out))
    new_params, new_momentum = update(
        lax.axis_size(("y_far", "z_far", "z_near")), near, parts, outer_params, momentum, fragment
    )
    return (moe_out, new_params, new_momentum)


def solution(mesh):
    reps, exps = mesh.devices.shape
    fine = Mesh(
        mesh.devices.reshape(reps // (RADIX * RADIX), RADIX, RADIX, exps // 2, 2),
        ("y_far", "z_far", "z_near", "chip", "core"),
    )
    rep = ("y_far", "z_far", "z_near")
    exp = ("chip", "core")
    return jax.shard_map(
        shards,
        mesh=fine,
        in_specs=(
            P(rep + exp, None),
            P(rep + exp, None),
            P(rep + exp, None),
            P(exp, None, None),
            P(exp, None, None),
            P(exp, None, None),
            P(rep, exp, None),
            P(rep, exp, None),
            P(None, exp, None),
            P(exp, None),
            P(),
        ),
        out_specs=(P(rep + exp, None), P(exp, None), P(exp, None)),
        check_vma=False,
    )
```

```python
import functools

import jax
import jax.numpy as jnp
from jax import lax
from jax.experimental import pallas as pl
from jax.experimental.pallas import tpu as pltpu
from jax.sharding import Mesh
from jax.sharding import PartitionSpec as P

CAP = 16
RADIX = 4

momentum_rate = 0.9
outer_rate = 0.7

ROUTE_PARAMS = pltpu.CompilerParams(vmem_limit_bytes=62 * 1024 * 1024)
EXPERT_PARAMS = pltpu.CompilerParams(vmem_limit_bytes=63 * 1024 * 1024)
PARAMS = pltpu.CompilerParams(vmem_limit_bytes=20 * 1024 * 1024)
VMEM = pl.BlockSpec(memory_space=pltpu.VMEM)
HBM = pl.BlockSpec(memory_space=pltpu.HBM)
SMEM = pl.BlockSpec(memory_space=pltpu.SMEM)


def route_kernel(experts, *refs):
    sources, (buffer_ref, combine_ref), targets, sems = refs[:3], refs[3:5], refs[5:8], refs[8]
    fetches = [
        pltpu.make_async_copy(source, target, sems.at[i])
        for i, (source, target) in enumerate(zip(sources, targets))
    ]
    for fetch in fetches:
        fetch.start()
    ids_ref, weights_ref, tokens_ref = targets
    topk, rows = ids_ref.shape
    fetches[0].wait()
    ids = ids_ref[...]
    fetches[1].wait()
    weights = weights_ref[...]
    expert = lax.broadcasted_iota(jnp.int32, (experts, rows), 0)
    named = jnp.zeros((experts, rows), jnp.float32)
    weight = jnp.zeros((experts, rows), jnp.float32)
    for k in range(topk):
        hit = ids[k : k + 1, :] == expert
        named = named + hit.astype(jnp.float32)
        weight = weight + jnp.where(hit, weights[k : k + 1, :], 0.0)
    earlier = lax.broadcasted_iota(jnp.int32, (rows, rows), 0) < lax.broadcasted_iota(
        jnp.int32, (rows, rows), 1
    )
    rank = jnp.dot(
        named.astype(jnp.bfloat16),
        earlier.astype(jnp.bfloat16),
        preferred_element_type=jnp.float32,
    ).astype(jnp.int32)
    rank = jnp.where(named > 0.5, rank, CAP)
    place = lax.broadcasted_iota(jnp.int32, (experts, CAP, rows), 1)
    chosen = rank[:, None, :] == place
    pick = jnp.where(chosen, 1.0, 0.0).reshape(experts * CAP, rows)
    combine_ref[...] = (
        jnp.where(chosen, jnp.broadcast_to(weight[:, None, :], chosen.shape), 0.0)
        .reshape(experts * CAP, rows)
        .astype(jnp.bfloat16)
    )
    fetches[2].wait()
    buffer_ref[...] = jnp.dot(
        pick.astype(jnp.bfloat16), tokens_ref[...], preferred_element_type=jnp.float32
    ).astype(jnp.bfloat16)


def route(tokens, expert_ids, route_weights, experts):
    rows, width = tokens.shape
    operands = (expert_ids.T, route_weights.T, tokens)
    return pl.pallas_call(
        functools.partial(route_kernel, experts),
        out_shape=(
            jax.ShapeDtypeStruct((experts * CAP, width), jnp.bfloat16),
            jax.ShapeDtypeStruct((experts * CAP, rows), jnp.bfloat16),
        ),
        in_specs=[HBM] * len(operands),
        scratch_shapes=[pltpu.VMEM(x.shape, x.dtype) for x in operands]
        + [pltpu.SemaphoreType.DMA((len(operands),))],
        compiler_params=ROUTE_PARAMS,
        name="route",
    )(*operands)


def expert_kernel(rows_hbm, *refs):
    sources, out_ref, targets, sems = refs[:6], refs[6], refs[7:11], refs[11]
    rows_ref, gate_ref, up_ref, down_ref = targets
    half = gate_ref.shape[1] // 2
    moves = [(rows_hbm, rows_ref)]
    for kind, target in enumerate((gate_ref, up_ref, down_ref)):
        for side in range(2):
            span = pl.ds(side * half, half)
            source = sources[3 * side + kind].at[0]
            moves.append((source, target.at[span] if kind == 2 else target.at[:, span]))
    fetches = [
        pltpu.make_async_copy(source, target, sems.at[i])
        for i, (source, target) in enumerate(moves)
    ]
    for fetch in fetches[:5]:
        fetch.start()
    for fetch in fetches[:3]:
        fetch.wait()
    for fetch in fetches[5:]:
        fetch.start()
    rows = rows_ref[...]
    gate = jnp.dot(rows, gate_ref[...], preferred_element_type=jnp.float32)
    for fetch in fetches[3:5]:
        fetch.wait()
    up = jnp.dot(rows, up_ref[...], preferred_element_type=jnp.float32)
    hidden = (gate / (1.0 + jnp.exp(-gate)) * up).astype(jnp.bfloat16)
    for fetch in fetches[5:]:
        fetch.wait()
    out_ref[...] = jnp.dot(hidden, down_ref[...], preferred_element_type=jnp.float32).astype(
        jnp.bfloat16
    )


def expert_rows(rows, own, other):
    operands = (rows,) + own + other
    _, width, half = own[0].shape
    wide = pltpu.VMEM((width, 2 * half), jnp.bfloat16)
    return pl.pallas_call(
        expert_kernel,
        in_specs=[HBM] * len(operands),
        out_shape=jax.ShapeDtypeStruct(rows.shape, jnp.bfloat16),
        scratch_shapes=[
            pltpu.VMEM(rows.shape, rows.dtype),
            wide,
            wide,
            pltpu.VMEM((2 * half, width), jnp.bfloat16),
            pltpu.SemaphoreType.DMA((len(operands),)),
        ],
        compiler_params=EXPERT_PARAMS,
        name="expert_rows",
    )(*operands)


def combine_kernel(combine_ref, rows_ref, out_ref):
    out_ref[...] = lax.dot_general(
        combine_ref[...],
        rows_ref[...],
        (((0,), (0,)), ((), ())),
        preferred_element_type=jnp.float32,
    ).astype(jnp.bfloat16)


def combine_rows(combine, rows):
    return pl.pallas_call(
        combine_kernel,
        out_shape=jax.ShapeDtypeStruct((combine.shape[1], rows.shape[1]), jnp.bfloat16),
        compiler_params=PARAMS,
        name="combine_rows",
    )(combine, rows)


def dequant_kernel(place_ref, values_ref, scales_ref, *out_refs):
    rows, width = out_refs[0].shape
    blocks = scales_ref.shape[0]
    column = lax.broadcasted_iota(jnp.int32, (blocks, width), 1) // (width // blocks)
    spread = (column == lax.broadcasted_iota(jnp.int32, (blocks, width), 0)).astype(jnp.bfloat16)
    scales = scales_ref[...]
    high = scales.astype(jnp.bfloat16)
    rest = scales - high.astype(jnp.float32)
    middle = rest.astype(jnp.bfloat16)
    low = (rest - middle.astype(jnp.float32)).astype(jnp.bfloat16)
    wide = sum(
        lax.dot_general(
            part, spread, (((0,), (0,)), ((), ())), preferred_element_type=jnp.float32
        )
        for part in (high, middle, low)
    )
    whole = (values_ref[0].astype(jnp.float32) * wide).astype(jnp.bfloat16)
    for place in range(RADIX):
        block = whole[place * rows : (place + 1) * rows]
        for step, out_ref in enumerate(out_refs):

            @pl.when((place_ref[0] + step) % RADIX == place)
            def _():
                out_ref[...] = block


def dequant(place, values, scales):
    _, rows, width = values.shape
    part = jax.ShapeDtypeStruct((rows // RADIX, width), jnp.bfloat16)
    return pl.pallas_call(
        dequant_kernel,
        in_specs=[SMEM, VMEM, VMEM],
        out_shape=(part,) * RADIX,
        compiler_params=PARAMS,
        name="dequant",
    )(place, values, scales[0].T)


def add_kernel(*refs):
    refs[-1][...] = sum(ref[...].astype(jnp.float32) for ref in refs[:-1]).astype(jnp.bfloat16)


def add_parts(parts):
    return pl.pallas_call(
        add_kernel,
        out_shape=jax.ShapeDtypeStruct(parts[0].shape, jnp.bfloat16),
        compiler_params=PARAMS,
        name="add_parts",
    )(*parts)


def total_kernel(parts_ref, out_ref):
    total = jnp.sum(parts_ref[...].astype(jnp.float32), axis=0).astype(jnp.bfloat16)
    out_ref[...] = jnp.broadcast_to(total[None], out_ref.shape)


def total_spread(parts):
    return pl.pallas_call(
        total_kernel,
        out_shape=jax.ShapeDtypeStruct((RADIX,) + parts.shape[1:], jnp.bfloat16),
        compiler_params=PARAMS,
        name="total_spread",
    )(parts)


def update_kernel(replicas, fragment_ref, totals_ref, base_ref, momentum_ref, params_out, momentum_out):
    pieces, rows, _ = totals_ref.shape
    for piece in range(pieces):
        at = pl.ds(piece * rows, rows)
        delta = totals_ref[piece].astype(jnp.float32) / replicas
        new_momentum = momentum_rate * momentum_ref[at, :] + delta
        momentum_out[at, :] = new_momentum
        params_out[at, :] = base_ref[0, at, :] - outer_rate * (
            delta + momentum_rate * new_momentum
        )


def update(replicas, totals, outer_params, momentum, fragment):
    shape = momentum.shape

    def whole(block):
        return pl.BlockSpec(block, lambda i, fragment_ref: (0,) * len(block))

    return pl.pallas_call(
        functools.partial(update_kernel, replicas),
        grid_spec=pltpu.PrefetchScalarGridSpec(
            num_scalar_prefetch=1,
            grid=(1,),
            in_specs=[
                whole(totals.shape),
                pl.BlockSpec((1,) + shape, lambda i, fragment_ref: (fragment_ref[0], 0, 0)),
                whole(shape),
            ],
            out_specs=(whole(shape), whole(shape)),
        ),
        out_shape=(
            jax.ShapeDtypeStruct(shape, jnp.float32),
            jax.ShapeDtypeStruct(shape, jnp.float32),
        ),
        compiler_params=PARAMS,
        name="update",
    )(fragment, totals, outer_params, momentum)


def shift(part, axis, step):
    size = lax.axis_size(axis)
    return lax.ppermute(part, axis, [(i, (i + step) % size) for i in range(size)])


def scatter_stage(parts, axis):
    return [parts[0]] + [shift(parts[step], axis, step) for step in range(1, RADIX)]


def place_on(axis):
    return lax.axis_index(axis).astype(jnp.int32).reshape(1)


def exchange(rows, experts):
    width = rows.shape[1]
    return lax.all_to_all(
        rows.reshape(experts, CAP, width), "chip", split_axis=0, concat_axis=0, tiled=True
    ).reshape(experts * CAP, width)


def shards(
    tokens,
    expert_ids,
    route_weights,
    w_gate,
    w_up,
    w_down,
    pseudo_values,
    block_scales,
    outer_params,
    momentum,
    fragment,
):
    experts = lax.axis_size("chip")
    buffer, combine = route(tokens, expert_ids, route_weights, experts)
    mine = exchange(buffer, experts)
    own = (w_gate, w_up, w_down)
    near = place_on("z_near")
    part = add_parts(scatter_stage(dequant(near, pseudo_values, block_scales), "z_near"))
    part, down = lax.optimization_barrier((part, w_down))
    other = (shift(w_gate, "core", 1), shift(w_up, "core", 1), shift(down, "core", 1))
    apart = shift(part, "y_far", 1)
    mine, part = lax.optimization_barrier((mine, part))
    rows = expert_rows(mine, own, other)
    rows, apart = lax.optimization_barrier((rows, apart))
    part = add_parts([part, apart])
    returned = exchange(rows, experts)
    spread = total_spread(lax.all_gather(part, "z_far", axis=0))
    returned, spread = lax.optimization_barrier((returned, spread))
    totals = lax.all_to_all(spread, "z_near", split_axis=0, concat_axis=0, tiled=True)
    moe_out = combine_rows(combine, returned)
    new_params, new_momentum = update(
        lax.axis_size(("y_far", "z_far", "z_near")), totals, outer_params, momentum, fragment
    )
    return (moe_out, new_params, new_momentum)


def solution(mesh):
    reps, exps = mesh.devices.shape
    fine = Mesh(
        mesh.devices.reshape(reps // (RADIX * RADIX), RADIX, RADIX, exps // 2, 2),
        ("y_far", "z_far", "z_near", "chip", "core"),
    )
    rep = ("y_far", "z_far", "z_near")
    exp = ("chip", "core")
    return jax.shard_map(
        shards,
        mesh=fine,
        in_specs=(
            P(rep + exp, None),
            P(rep + exp, None),
            P(rep + exp, None),
            P(exp, None, None),
            P(exp, None, None),
            P(exp, None, None),
            P(rep, exp, None),
            P(rep, exp, None),
            P(None, exp, None),
            P(exp, None),
            P(),
        ),
        out_specs=(P(rep + exp, None), P(exp, None), P(exp, None)),
        check_vma=False,
    )
```
